32 devices in a mesh: wide: 8 (over z, y), narrow: 4 (over x, core).
Axes of the slice: x: 2, y: 2, z: 4, core: 2. Of those that a mesh axis runs over, the one named last changes fastest.
Arguments:
- images: bfloat16 [8192, 4, 4, 512], P(('wide', 'narrow')), may hold values from -6 to 6
- labels: int32 [8192], P(('wide', 'narrow')), may hold values from 0 to 9
- class_weight: int32 [10], replicated, may hold values from 1 to 5
- basis_index: int32 [2, 128], replicated, may hold values from 1 to 511, as said below
- atom_mask: int32 [2, 8, 4608, 128], P(None, 'wide', 'narrow'), may hold values 0 or 1
- conv_weight: float32 [2, 4608, 512], P(None, 'narrow'), may hold values from -0.09375 to 0.09375
- conv_momentum: float32 [2, 4608, 512], P(None, 'narrow'), may hold values from -0.0017089844 to 0.0017089844
- batch_norm_params: float32 [4, 512], replicated, may hold values from 0.5 to 1.5
- norm_first: float32 [4, 512], replicated, may hold values from -0.00030517578 to 0.00030517578
- norm_second: float32 [4, 512], replicated, may hold values from 4.8828126e-11 to 1.953125e-10
- head_weight: float32 [10, 512], replicated, may hold values from -0.25 to 0.25
- head_first: float32 [10, 512], replicated, may hold values from -0.0034179688 to 0.0034179688
- head_second: float32 [10, 512], replicated, may hold values from 3e-06 to 1.2e-05
- head_bias: float32 [10], replicated, may hold values from -3 to 3
- bias_first: float32 [10], replicated, may hold values from -0.0048828125 to 0.0048828125
- bias_second: float32 [10], replicated, may hold values from 3e-06 to 1.2e-05
Outputs:
- loss_sum: float32 [], replicated
- weight_total: float32 [], replicated
- new_conv_weight: float32 [2, 4608, 512], P(None, 'narrow')
- new_conv_momentum: float32 [2, 4608, 512], P(None, 'narrow')
- conv_copy: bfloat16 [2, 4608, 512], P(None, 'narrow')
- new_norm_vectors: float32 [4, 512], replicated
- new_norm_first: float32 [4, 512], replicated
- bottom_second: float32 [2, 512], replicated
- top_second: float32 [2, 512], replicated
- new_head_weight: float32 [10, 512], replicated
- new_head_first: float32 [10, 512], replicated
- new_head_second: float32 [10, 512], replicated
- new_head_bias: float32 [10], replicated
- new_bias_first: float32 [10], replicated
- new_bias_second: float32 [10], replicated
The draws below stay inside these ranges and needn't reach their ends.
Inputs may be any that keep to these rules, and one draw needn't show every extreme that they name: `basis_index`: each row holds 128 distinct frequencies.
All inputs are finite; a program needn't handle non-finite values. No bound on the sum of `atom_mask` on one device may be relied on, other than what follows from the above.
Results may differ from the reference program's by a relative error of at most 0.0017.
The reference program's roundings to bfloat16 on the way count: a program that leaves them out, or rounds other values in their place, can miss the bound.
Values may be sent and summed in bfloat16 or wider, within the bound.
No kernel may reach another device: no remote copies, remote signals or barrier semaphores. Data moves between devices by JAX's collectives and lax.ppermute only.
A program may use at most 320 MiB of HBM per device.

```python
import math
import jax
import jax.numpy as jnp
from jax import lax

C = 512
CLASSES = 10
SIDE = 4
RANK = 128
NS_STEPS = 5
STEP = 5
K9 = 4608
IMAGES = 8192
N_WIDE = 8


def draw_basis_index(key, part):
    key = jax.random.fold_in(key, 7)
    rows = []
    for layer in range(2):
        order = jax.random.permutation(jax.random.fold_in(key, layer), C - 3).astype(jnp.int32) + 2
        ends = jnp.array([1, C - 1], jnp.int32)
        rows.append(jnp.concatenate([ends, order[:RANK - 2]]))
    return jnp.stack(rows)


def place_ends(result, rng, smallest, top_value):
    longest = result.shape.index(max(result.shape))
    spots = []
    for shift in (0, 1):
        where = [jax.random.randint(jax.random.fold_in(rng, axis), (), 0, length) for axis, length in enumerate(result.shape)]
        where[longest] = (where[longest] + shift) % result.shape[longest]
        spots.append(tuple(where))
    return result.at[spots[0]].set(smallest).at[spots[1]].set(top_value)


def level_of(rng, shape, cuts, least, largest):
    factor_of = 1.0
    for dim, parts in cuts:
        draws = jax.random.uniform(jax.random.fold_in(jax.random.fold_in(rng, 6), dim), (parts,), jnp.float32, least / len(cuts), largest / len(cuts))
        factor_of = factor_of * jnp.repeat(jnp.exp(draws), shape[dim] // parts).reshape((-1,) + (1,) * (len(shape) - 1 - dim))
    return factor_of


def normal_values(own_key, extent, scale, limit, shards=(), kind=jnp.bfloat16):
    result = jax.random.normal(own_key, extent, jnp.float32) * scale
    if len(shards) > 0:
        result = level_of(own_key, extent, shards, -0.22, 0.18) * result
    return jnp.clip(result, min=-limit, max=limit).astype(kind)


def setup_inputs(seed: int = 0) -> dict:
    streams_of = jax.random.split(jax.random.key(seed), 17)
    images = normal_values(streams_of[0], (IMAGES, SIDE, SIDE, C), 1.0, 6.0, ((0, 32),))
    labels = place_ends(jax.random.randint(streams_of[1], (IMAGES,), 0, CLASSES), jax.random.fold_in(streams_of[1], 1), 0, CLASSES - 1).astype(jnp.int32)
    class_weight = place_ends(jax.random.randint(streams_of[2], (CLASSES,), 1, 6), jax.random.fold_in(streams_of[2], 1), 1, 5).astype(jnp.int32)
    basis_index = draw_basis_index(jax.random.fold_in(streams_of[16], 71), 0)
    atom_mask = place_ends((jax.random.randint(streams_of[4], (2, N_WIDE, K9, RANK), 0, 2) < 1).astype(jnp.int32), jax.random.fold_in(streams_of[4], 1), 0, 1)
    conv_weight = normal_values(streams_of[5], (2, K9, C), K9 ** -0.5, 0.09375, ((1, 4),), jnp.float32)
    conv_momentum = normal_values(streams_of[6], (2, K9, C), (0.01 / IMAGES ** 0.5), 0.0017089844, ((1, 4),), jnp.float32)
    batch_norm_params = jnp.clip(jax.random.uniform(streams_of[7], (4, C), jnp.float32, 0.5, 1.5), 0.5, 1.5)
    norm_first = normal_values(streams_of[8], (4, C), (0.002 / IMAGES ** 0.5), 0.00030517578, (), jnp.float32)
    norm_second = jnp.clip(jnp.exp(jax.random.uniform(streams_of[9], (4, C), jnp.float32, math.log(4.8828125570610226e-11), math.log(1.953125022824409e-10))), 4.8828125570610226e-11, 1.953125022824409e-10)
    head_weight = normal_values(streams_of[10], (CLASSES, C), C ** -0.5, 0.25, (), jnp.float32)
    head_first = normal_values(streams_of[11], (CLASSES, C), (0.02 / IMAGES ** 0.5), 0.0034179688, (), jnp.float32)
    head_second = jnp.clip(jnp.exp(jax.random.uniform(streams_of[12], (CLASSES, C), jnp.float32, math.log(3.000000106112566e-06), math.log(1.2000000424450263e-05))), 3.000000106112566e-06, 1.2000000424450263e-05)
    head_bias = normal_values(streams_of[13], (CLASSES,), 0.5, 3.0, (), jnp.float32)
    bias_first = normal_values(streams_of[14], (CLASSES,), (0.03 / IMAGES ** 0.5), 0.0048828125, (), jnp.float32)
    bias_second = jnp.clip(jnp.exp(jax.random.uniform(streams_of[15], (CLASSES,), jnp.float32, math.log(3.000000106112566e-06), math.log(1.2000000424450263e-05))), 3.000000106112566e-06, 1.2000000424450263e-05)
    return dict(images=images, labels=labels, class_weight=class_weight, basis_index=basis_index, atom_mask=atom_mask, conv_weight=conv_weight, conv_momentum=conv_momentum, batch_norm_params=batch_norm_params, norm_first=norm_first, norm_second=norm_second, head_weight=head_weight, head_first=head_first, head_second=head_second, head_bias=head_bias, bias_first=bias_first, bias_second=bias_second)


@jax.custom_vjp
def low(v):
    return lax.optimization_barrier(v.astype(jnp.bfloat16)).astype(jnp.float32)

@jax.custom_vjp
def low_back(v):
    return v

def low_keep(v):
    return (low(v), None)

def low_pass(kept, grad):
    return (grad,)

def back_keep(v):
    return (v, None)

def back_low(kept, grad):
    return (low(grad),)
low.defvjp(low_keep, low_pass)
low_back.defvjp(back_keep, back_low)
highest = lax.Precision.HIGHEST
norm_eps = 1e-05
smooth = 0.1
ns_a, ns_b, ns_c = (3.4445, -4.775, 2.0315)

def patches_of(field):
    count, side, _, width = field.shape
    padded = jnp.pad(field, ((0, 0), (1, 1), (1, 1), (0, 0)))
    pieces = [padded[:, a:a + side, b:b + side, :] for a in range(3) for b in range(3)]
    return jnp.concatenate(pieces, axis=3).reshape(count * side * side, 9 * width)

def normed(hidden_state, norm_gain, norm_shift):
    batch_mean = lax.optimization_barrier(jnp.mean(hidden_state, axis=(0, 1)))
    var = lax.optimization_barrier(jnp.mean(jnp.square(hidden_state - batch_mean), axis=(0, 1)))
    return norm_gain * (hidden_state - batch_mean) * lax.rsqrt(var + norm_eps) + norm_shift

def forward(copies, vectors, head_w, head_b, field, labels, weights_each, total):
    rounded = low(copies)

    def conv_all(inputs, layer):

        def one_group(pair):
            return jnp.dot(patches_of(pair[0]), pair[1][layer], precision=highest, preferred_element_type=jnp.float32)
        return lax.map(jax.checkpoint(one_group), (inputs, rounded))
    first_hidden = low_back(conv_all(field, 0))
    z1 = low(jax.nn.silu(normed(first_hidden, vectors[0], vectors[1])))
    second_hidden = low_back(conv_all(z1.reshape(field.shape), 1))
    res = normed(second_hidden, vectors[2], vectors[3]) + field.reshape(second_hidden.shape)
    act = jax.nn.silu(res)
    pooled = low(lax.optimization_barrier(jnp.mean(act.reshape(-1, SIDE * SIDE, C), axis=1)))
    logits = jnp.dot(pooled, low(head_w).T, precision=highest, preferred_element_type=jnp.float32) + head_b
    logp = jax.nn.log_softmax(logits, axis=-1)
    target = (1.0 - smooth) * jax.nn.one_hot(labels, CLASSES, dtype=jnp.float32) + smooth / CLASSES
    per = -lax.optimization_barrier(jnp.sum(target * logp, axis=-1))
    loss_sum = jnp.sum(weights_each * per)
    return (loss_sum / total, loss_sum)

def cosine_rows(index):
    cols = jnp.arange(C, dtype=jnp.float32)
    freq = index.astype(jnp.float32)[:, None]
    return jnp.sqrt(2.0 / C) * jnp.cos(jnp.pi * freq * (2.0 * cols[None, :] + 1.0) / (2.0 * C))

def orthogonalize(moment):
    x = moment / (jnp.sqrt(jnp.sum(moment * moment)) + 1e-07)
    for step in range(NS_STEPS):
        gram = jnp.dot(x.T, x, precision=highest)
        poly = ns_b * gram + ns_c * jnp.dot(gram, gram, precision=highest)
        x = ns_a * x + jnp.dot(x, poly, precision=highest)
    return x

def adamw(param, grad, first, second, rate, decay):
    first = 0.9 * first + 0.1 * grad
    second = 0.999 * second + 0.001 * grad * grad
    mhat = first / (1.0 - 0.9 ** STEP)
    vhat = second / (1.0 - 0.999 ** STEP)
    param = param - rate * (mhat / (jnp.sqrt(vhat) + 1e-08) + decay * param)
    return (param, first, second)

def reference(images, labels, class_weight, basis_index, atom_mask, conv_weight, conv_momentum, batch_norm_params, norm_first, norm_second, head_weight, head_first, head_second, head_bias, bias_first, bias_second):
    field = images.astype(jnp.float32).reshape(N_WIDE, -1, SIDE, SIDE, C)
    weights_each = class_weight.astype(jnp.float32)[labels]
    total = jnp.sum(weights_each)
    copies = jnp.broadcast_to(conv_weight, (N_WIDE,) + conv_weight.shape)

    def objective(cw, vec, hw, hb):
        return forward(cw, vec, hw, hb, field, labels, weights_each, total)
    value, pull, loss_sum = jax.vjp(objective, copies, batch_norm_params, head_weight, head_bias, has_aux=True)
    grad_conv, grad_vec, grad_head, grad_bias = pull(jnp.float32(1.0))
    weights_out, moments_out = ([], [])
    for layer in range(2):
        basis = cosine_rows(basis_index[layer])
        coef = jnp.einsum('gkc,rc->gkr', grad_conv[:, layer], basis, precision=highest)
        kept = lax.optimization_barrier(jnp.sum(coef * atom_mask[layer].astype(jnp.float32), axis=0))
        rebuilt = jnp.dot(kept, basis, precision=highest)
        moment = 0.95 * conv_momentum[layer] + rebuilt
        ortho = orthogonalize(moment)
        weights_out.append(conv_weight[layer] * (1.0 - 0.1 * 0.01) - 0.1 * 3.0 * ortho)
        moments_out.append(moment)
    new_w = jnp.stack(weights_out)
    new_m = jnp.stack(moments_out)
    vec, vec_m, vec_v = adamw(batch_norm_params, grad_vec, norm_first, norm_second, 0.3, 0.0)
    hw, hw_m, hw_v = adamw(head_weight, grad_head, head_first, head_second, 0.03, 0.01)
    hb, hb_m, hb_v = adamw(head_bias, grad_bias, bias_first, bias_second, 0.3, 0.0)
    return (loss_sum, total, new_w, new_m, new_w.astype(jnp.bfloat16), vec, vec_m, vec_v[:2], vec_v[2:], hw, hw_m, hw_v, hb, hb_m, hb_v)
```

```python
import functools

import jax
import jax.numpy as jnp
from jax import lax
from jax.experimental import pallas as pl
from jax.experimental.pallas import tpu as pltpu
from jax.sharding import PartitionSpec as P

SIDE = 4
PIX = SIDE * SIDE
TAPS = 9
NS_STEPS = 5
STEP = 5

f32 = jnp.float32
bf16 = jnp.bfloat16
highest = lax.Precision.HIGHEST
norm_eps = 1e-05
smooth = 0.1
ns_a, ns_b, ns_c = (3.4445, -4.775, 2.0315)
MIB = 1 << 20

ANY = pl.BlockSpec(memory_space=pl.ANY)
VMEM = pl.BlockSpec(memory_space=pltpu.VMEM)
SMEM = pl.BlockSpec(memory_space=pltpu.SMEM)


def out_taps(pixel):
    p, q = divmod(pixel, SIDE)
    found = []
    for tap in range(TAPS):
        a, b = divmod(tap, 3)
        pp, qq = p + a - 1, q + b - 1
        if 0 <= pp < SIDE and 0 <= qq < SIDE:
            found.append((tap, pp * SIDE + qq))
    return found


def in_taps(pixel):
    found = []
    for out in range(PIX):
        for tap, source in out_taps(out):
            if source == pixel:
                found.append((tap, out))
    return found


def sigma_of(value):
    return 0.5 * jnp.tanh(0.5 * value) + 0.5


def loads(source, target, sems):
    copies = [
        pltpu.make_async_copy(source.at[i], target.at[i], sems.at[i])
        for i in range(target.shape[0])
    ]
    for copy in copies:
        copy.start()
    return copies


def weight_loads(me_ref, pieces, target, sems):
    me = me_ref[0]
    copies = []
    rows = pieces[0].shape[0]
    for k, piece in enumerate(pieces):
        start = pl.multiple_of((me ^ k) * rows, rows)
        copies.append(pltpu.make_async_copy(piece, target.at[pl.ds(start, rows)], sems.at[k]))
        copies[-1].start()
    return copies


def block_moments(block):
    mean = jnp.sum(block, axis=0, keepdims=True) * (1.0 / block.shape[0])
    return mean, jnp.sum(jnp.square(block - mean), axis=0, keepdims=True)


def store_moments(stats_ref, parts, rows, extra):
    mean = sum(m for m, _ in parts) * (1.0 / len(parts))
    square = sum(s for _, s in parts) + rows * sum(jnp.square(m - mean) for m, _ in parts)
    stats_ref[0:1] = mean
    stats_ref[1:2] = square
    stats_ref[2:3] = extra
    stats_ref[3:8] = jnp.zeros((5, mean.shape[1]), f32)


def conv_pixel(source, weight, pixel, width):
    total = None
    for tap, read in out_taps(pixel):
        part = jnp.dot(
            source[read], weight[tap * width : (tap + 1) * width], preferred_element_type=f32
        )
        total = part if total is None else total + part
    return total


def conv_first_kernel(
    me_ref, extra_ref, x_any, w0, w1, w2, w3, hid_any, stats_ref, x_v, w_v, hid_v, xs, ws, os
):
    width = x_v.shape[2]
    wait_w = weight_loads(me_ref, (w0, w1, w2, w3), w_v, ws)
    wait_x = loads(x_any, x_v, xs)
    for copy in wait_w + wait_x:
        copy.wait()
    parts, sends = [], []
    for pixel in range(PIX):
        block = conv_pixel(x_v, w_v, pixel, width)
        hid_v[pixel] = block
        sends.append(pltpu.make_async_copy(hid_v.at[pixel], hid_any.at[pixel], os.at[pixel]))
        sends[-1].start()
        parts.append(block_moments(block))
    store_moments(stats_ref, parts, x_v.shape[1], extra_ref[...])
    for copy in sends:
        copy.wait()


def norm_rows(stats_ref, pixel_count):
    mean = stats_ref[0:1]
    return mean, lax.rsqrt(stats_ref[1:2] * (1.0 / pixel_count) + norm_eps)


def conv_second_kernel(
    pixel_count,
    me_ref,
    extra_ref,
    stats_in,
    params,
    h_any,
    w0,
    w1,
    w2,
    w3,
    hid_any,
    z_any,
    stats_ref,
    h_v,
    z_v,
    w_v,
    hid_v,
    hs,
    ws,
    os,
    zs,
):
    width = h_v.shape[2]
    wait_h = loads(h_any, h_v, hs)
    wait_w = weight_loads(me_ref, (w0, w1, w2, w3), w_v, ws)
    mean, scale = norm_rows(stats_in, pixel_count)
    gain = params[0:1] * scale
    shift = params[1:2]
    sends = []

    def activate(pixel):
        wait_h[pixel].wait()
        value = (h_v[pixel] - mean) * gain + shift
        z_v[pixel] = (value * sigma_of(value)).astype(bf16)
        sends.append(pltpu.make_async_copy(z_v.at[pixel], z_any.at[pixel], zs.at[pixel]))
        sends[-1].start()

    parts = []
    for pixel in range(2 * SIDE):
        activate(pixel)
    for copy in wait_w:
        copy.wait()
    for pixel in range(PIX):
        if pixel + SIDE + 1 < PIX and pixel + SIDE + 1 >= 2 * SIDE:
            activate(pixel + SIDE + 1)
        block = conv_pixel(z_v, w_v, pixel, width)
        hid_v[pixel] = block
        sends.append(pltpu.make_async_copy(hid_v.at[pixel], hid_any.at[pixel], os.at[pixel]))
        sends[-1].start()
        parts.append(block_moments(block))
    store_moments(stats_ref, parts, h_v.shape[1], extra_ref[...])
    for copy in sends:
        copy.wait()


def head_kernel(
    pixel_count,
    classes,
    stats_in,
    params,
    head_ref,
    bias_ref,
    label_ref,
    class_ref,
    h_any,
    x_any,
    slope_any,
    dp_ref,
    sums_ref,
    aux_ref,
    h_v,
    x_v,
    slope_v,
    pool_v,
    s1_v,
    s2_v,
    hs,
    xs,
    os,
):
    count, width = h_v.shape[1:]
    rows = 32
    chunks = count // rows

    def chunk_copy(source, target, sems, i):
        start = pl.multiple_of(i * rows, rows)
        return pltpu.make_async_copy(
            source.at[:, pl.ds(start, rows)], target.at[:, pl.ds(start, rows)], sems.at[i]
        )

    for i in range(chunks):
        chunk_copy(h_any, h_v, hs, i).start()
        chunk_copy(x_any, x_v, xs, i).start()
    mean, scale = norm_rows(stats_in, pixel_count)
    gain, shift = params[2:3], params[3:4]

    def body(i, carry):
        chunk_copy(h_any, h_v, hs, i).wait()
        chunk_copy(x_any, x_v, xs, i).wait()
        here = pl.ds(pl.multiple_of(i * rows, rows), rows)
        for lane in range(0, width, 128):
            cut = slice(lane, lane + 128)
            m, r, g, s = mean[:, cut], scale[:, cut], gain[:, cut], shift[:, cut]
            pool = jnp.zeros((rows, 128), f32)
            s1 = jnp.zeros((rows, 128), f32)
            s2 = jnp.zeros((rows, 128), f32)
            for pixel in range(PIX):
                xh = (h_v[pixel, here, cut] - m) * r
                res = (g * xh + s) + x_v[pixel, here, cut].astype(f32)
                sig = sigma_of(res)
                act = res * sig
                slope = sig + act * (1.0 - sig)
                slope_v[pixel, here, cut] = slope
                pool = pool + act
                s1 = s1 + slope
                s2 = s2 + slope * xh
            pool_v[here, cut] = (pool * (1.0 / PIX)).astype(bf16)
            s1_v[here, cut] = s1
            s2_v[here, cut] = s2
        chunk_copy(slope_v, slope_any, os, i).start()
        return carry

    lax.fori_loop(0, chunks, body, 0)
    pooled = pool_v[...]
    head = head_ref[...]
    logits = (
        lax.dot_general(pooled, head, (((1,), (1,)), ((), ())), preferred_element_type=f32)
        + bias_ref[...]
    )
    lane_index = lax.broadcasted_iota(jnp.int32, logits.shape, 1)
    valid = lane_index < classes
    onehot = (lane_index == label_ref[...]).astype(f32)
    weight_each = jnp.sum(onehot * class_ref[...], axis=1, keepdims=True)
    top = jnp.max(jnp.where(valid, logits, -jnp.inf), axis=1, keepdims=True)
    moved = jnp.where(valid, logits - top, 0.0)
    powers = jnp.where(valid, jnp.exp(moved), 0.0)
    total = jnp.sum(powers, axis=1, keepdims=True)
    logp = jnp.where(valid, moved - jnp.log(total), 0.0)
    target = jnp.where(valid, (1.0 - smooth) * onehot + smooth / classes, 0.0)
    per_image = -jnp.sum(target * logp, axis=1, keepdims=True)
    loss = jnp.sum(weight_each * per_image, axis=0, keepdims=True)
    weight_total = stats_in[2:3, 0:1]
    dlogits = weight_each * (powers / total - target) / weight_total
    dp = (
        jnp.dot(dlogits, head.astype(f32), precision=highest, preferred_element_type=f32)
        * (1.0 / PIX)
    )
    dp_ref[...] = dp
    sums_ref[0:1] = jnp.sum(dp * s1_v[...], axis=0, keepdims=True)
    sums_ref[1:2] = jnp.sum(dp * s2_v[...], axis=0, keepdims=True)
    sums_ref[2:8] = jnp.zeros((6, width), f32)
    head_grad = lax.dot_general(
        dlogits,
        pooled.astype(f32),
        (((0,), (0,)), ((), ())),
        precision=highest,
        preferred_element_type=f32,
    )
    aux_ref[0:16] = head_grad[0:16]
    aux_ref[16:24] = jnp.zeros((8, width), f32)
    aux_ref[16:17, 0:128] = jnp.sum(dlogits, axis=0, keepdims=True)
    aux_ref[17:18, 0:128] = jnp.broadcast_to(loss, (1, 128))
    for i in range(chunks):
        chunk_copy(slope_v, slope_any, os, i).wait()


def second_grad_kernel(
    pixel_count,
    me_ref,
    stats1,
    stats2,
    sums2,
    params,
    dp_ref,
    h2_any,
    slope_any,
    h1_any,
    w0,
    w1,
    w2,
    w3,
    dh_any,
    dy_any,
    sums_ref,
    h2_v,
    slope_v,
    h1_v,
    w_v,
    dh_v,
    dy_v,
    as_,
    bs,
    cs,
    ws,
    os,
    ys,
):
    width = h2_v.shape[2]
    wait_h2 = loads(h2_any, h2_v, as_)
    wait_slope = loads(slope_any, slope_v, bs)
    wait_w = weight_loads(me_ref, (w0, w1, w2, w3), w_v, ws)
    wait_h1 = loads(h1_any, h1_v, cs)
    mean2, scale2 = norm_rows(stats2, pixel_count)
    outer = params[2:3] * scale2
    shift_part = sums2[0:1] * (1.0 / pixel_count)
    gain_part = sums2[1:2] * (1.0 / pixel_count) * scale2
    mean1, scale1 = norm_rows(stats1, pixel_count)
    gain1, shift1 = params[0:1], params[1:2]
    sends = []

    def hidden_grad(pixel):
        wait_h2[pixel].wait()
        wait_slope[pixel].wait()
        grad = dp_ref[...] * slope_v[pixel] - shift_part - (h2_v[pixel] - mean2) * gain_part
        dh_v[pixel] = (outer * grad).astype(bf16)
        sends.append(pltpu.make_async_copy(dh_v.at[pixel], dh_any.at[pixel], os.at[pixel]))
        sends[-1].start()

    for pixel in range(2 * SIDE):
        hidden_grad(pixel)
    for copy in wait_w:
        copy.wait()
    shift_sum = jnp.zeros((1, width), f32)
    gain_sum = jnp.zeros((1, width), f32)
    for pixel in range(PIX):
        if pixel + SIDE + 1 < PIX and pixel + SIDE + 1 >= 2 * SIDE:
            hidden_grad(pixel + SIDE + 1)
        total = None
        for tap, out in in_taps(pixel):
            part = lax.dot_general(
                dh_v[out],
                w_v[tap * width : (tap + 1) * width],
                (((1,), (1,)), ((), ())),
                preferred_element_type=f32,
            )
            total = part if total is None else total + part
        wait_h1[pixel].wait()
        xh = (h1_v[pixel] - mean1) * scale1
        value = gain1 * xh + shift1
        sig = sigma_of(value)
        grad = total * (sig * (1.0 + value * (1.0 - sig)))
        dy_v[pixel] = grad
        sends.append(pltpu.make_async_copy(dy_v.at[pixel], dy_any.at[pixel], ys.at[pixel]))
        sends[-1].start()
        shift_sum = shift_sum + jnp.sum(grad, axis=0, keepdims=True)
        gain_sum = gain_sum + jnp.sum(grad * xh, axis=0, keepdims=True)
    sums_ref[0:1] = shift_sum
    sums_ref[1:2] = gain_sum
    sums_ref[2:8] = jnp.zeros((6, width), f32)
    for copy in sends:
        copy.wait()


def coef_body(me_ref, grad_of, source_of, basis_ref, turned, coef_v, keep_any, send_any, sems):
    rank = basis_ref.shape[1] // 2
    width = basis_ref.shape[0]
    for pixel in range(PIX):
        both = jnp.dot(grad_of(pixel), basis_ref[...], preferred_element_type=f32)
        low = both[:, :rank] + both[:, rank:]
        top = low.astype(bf16)
        rest = (low - top.astype(f32)).astype(bf16)
        turned[pixel, :rank] = top.T
        turned[pixel, rank:] = rest.T
    part_width = coef_v.shape[2]
    for tap in range(TAPS):
        total = None
        for pixel in range(PIX):
            for t, read in out_taps(pixel):
                if t == tap:
                    part = jnp.dot(turned[pixel], source_of(read), preferred_element_type=f32)
                    total = part if total is None else total + part
        coef = total[:rank] + total[rank:]
        at = tap * width
        while at < (tap + 1) * width:
            j = at // part_width
            end = min((j + 1) * part_width, (tap + 1) * width)
            coef_v[j, :, at - j * part_width : end - j * part_width] = coef[
                :, at - tap * width : end - tap * width
            ]
            at = end
    me = me_ref[0]
    copies = []
    for slot in range(2):
        copies.append(
            pltpu.make_async_copy(coef_v.at[me ^ (2 * slot)], keep_any.at[slot], sems.at[slot])
        )
        copies.append(
            pltpu.make_async_copy(
                coef_v.at[me ^ (2 * slot + 1)], send_any.at[slot], sems.at[2 + slot]
            )
        )
    for copy in copies:
        copy.start()
    for copy in copies:
        copy.wait()


def coef_second_kernel(
    me_ref, basis_ref, dh_any, z_any, keep_any, send_any, dh_v, z_v, turned, coef_v, as_, bs, sems
):
    wait_dh = loads(dh_any, dh_v, as_)
    wait_z = loads(z_any, z_v, bs)
    done = set()

    def grad_of(pixel):
        wait_dh[pixel].wait()
        return dh_v[pixel]

    def source_of(pixel):
        if pixel not in done:
            done.add(pixel)
            wait_z[pixel].wait()
        return z_v[pixel]

    coef_body(me_ref, grad_of, source_of, basis_ref, turned, coef_v, keep_any, send_any, sems)


def coef_first_kernel(
    pixel_count,
    me_ref,
    basis_ref,
    stats1,
    sums1,
    params,
    dy_any,
    h1_any,
    x_any,
    keep_any,
    send_any,
    dy_v,
    h1_v,
    x_v,
    turned,
    coef_v,
    as_,
    bs,
    cs,
    sems,
):
    wait_dy = loads(dy_any, dy_v, as_)
    wait_h1 = loads(h1_any, h1_v, bs)
    wait_x = loads(x_any, x_v, cs)
    mean, scale = norm_rows(stats1, pixel_count)
    outer = params[0:1] * scale
    shift_part = sums1[0:1] * (1.0 / pixel_count)
    gain_part = sums1[1:2] * (1.0 / pixel_count) * scale
    done = set()

    def grad_of(pixel):
        wait_dy[pixel].wait()
        wait_h1[pixel].wait()
        grad = dy_v[pixel] - shift_part - (h1_v[pixel] - mean) * gain_part
        return (outer * grad).astype(bf16)

    def source_of(pixel):
        if pixel not in done:
            done.add(pixel)
            wait_x[pixel].wait()
        return x_v[pixel]

    coef_body(me_ref, grad_of, source_of, basis_ref, turned, coef_v, keep_any, send_any, sems)


def halves(value):
    top = value.astype(bf16)
    return top, (value - top.astype(f32)).astype(bf16)


def dot3(left, right, dims=(((1,), (0,)), ((), ()))):
    (a, b), (c, d) = left, right

    def dot(x, y):
        return lax.dot_general(x, y, dims, preferred_element_type=f32)

    return dot(a, c) + (dot(a, d) + dot(b, c))


CONTRACT_ROWS = (((0,), (0,)), ((), ()))
CONTRACT_COLUMNS = (((1,), (1,)), ((), ()))


def gram_parts_kernel(kept_ref, mom_ref, out_ref):
    kept = halves(kept_ref[...])
    width = mom_ref.shape[2]
    out_ref[:, :width] = dot3(kept, halves(mom_ref[0]))
    out_ref[:, width:] = dot3(kept, kept, CONTRACT_COLUMNS)


def muon_kernel(mom_gram_ref, parts_ref, basis_ref, out_ref, scale_ref):
    width = basis_ref.shape[1]
    basis = basis_ref[...]
    pair = halves(basis)
    mixed = 0.95 * parts_ref[:, :width] + 0.5 * dot3(halves(parts_ref[:, width:]), pair)
    side = dot3(halves(mixed), pair, CONTRACT_ROWS)
    gram = 0.9025 * mom_gram_ref[...] + (side + side.T)
    row = lax.broadcasted_iota(jnp.int32, gram.shape, 0)
    column = lax.broadcasted_iota(jnp.int32, gram.shape, 1)
    eye = (row == column).astype(f32)
    norm = jnp.sqrt(jnp.sum(gram * eye, keepdims=True)) + 1e-07
    inverse = 1.0 / norm
    scale_ref[...] = jnp.broadcast_to(inverse, scale_ref.shape)
    gram = gram * (inverse * inverse)
    chain = None
    for step in range(NS_STEPS):
        gram_pair = halves(gram)
        poly = ns_b * gram + ns_c * dot3(gram_pair, gram_pair)
        poly_pair = halves(poly)
        if chain is None:
            chain = poly + ns_a * eye
        else:
            chain = ns_a * chain + dot3(halves(chain), poly_pair)
        if step + 1 < NS_STEPS:
            turn = ns_a * gram + dot3(gram_pair, poly_pair)
            gram = ns_a * turn + dot3(halves(turn), poly_pair)
    out_ref[...] = chain


def update_kernel(kept_ref, basis_ref, chain_ref, scale_ref, mom_ref, w_ref, *refs):
    new_w, new_m, copy = refs[-3:]
    rebuilt = dot3(halves(kept_ref[...]), halves(basis_ref[...]), CONTRACT_ROWS)
    moment = 0.95 * mom_ref[0] + rebuilt
    new_m[0] = moment
    step = dot3(halves(moment), halves(chain_ref[...]))
    fresh = w_ref[0] * (1.0 - 0.1 * 0.01) - (0.1 * 3.0) * scale_ref[0:1, 0:1] * step
    new_w[0] = fresh
    copy[0] = fresh.astype(bf16)


def cosine_rows(index, width):
    cols = jnp.arange(width, dtype=f32)
    freq = index.astype(f32)[..., None]
    return jnp.sqrt(2.0 / width) * jnp.cos(jnp.pi * freq * (2.0 * cols + 1.0) / (2.0 * width))


def adamw(param, grad, first, second, rate, decay):
    first = 0.9 * first + 0.1 * grad
    second = 0.999 * second + 0.001 * grad * grad
    mhat = first / (1.0 - 0.9**STEP)
    vhat = second / (1.0 - 0.999**STEP)
    param = param - rate * (mhat / (jnp.sqrt(vhat) + 1e-08) + decay * param)
    return (param, first, second)


def swap(value, axis, bit):
    size = lax.axis_size(axis)
    return lax.ppermute(value, axis, [(i, i ^ bit) for i in range(size)])


def axis_bits(axis):
    bit = 1
    while bit < lax.axis_size(axis):
        yield axis, bit
        bit *= 2


def all_bits():
    return list(axis_bits("narrow")) + list(axis_bits("wide"))


def sum_all(value):
    for axis, bit in all_bits():
        value = value + swap(value, axis, bit)
    return value


def merge_moments(stats, count):
    for axis, bit in all_bits():
        other = swap(stats, axis, bit)
        gap = stats[0] - other[0]
        stats = jnp.stack(
            [
                0.5 * (stats[0] + other[0]),
                stats[1] + other[1] + gap * gap * (0.5 * count),
                stats[2] + other[2],
            ]
            + [stats[i] for i in range(3, 8)]
        )
        count = 2 * count
    return stats


def sum_wide(value):
    where = lax.axis_index("wide")
    bits = [bit for _, bit in axis_bits("wide")]
    for bit in bits:
        half = value.shape[0] // 2
        mine = jnp.where((where & bit) != 0, half, 0)
        send = lax.dynamic_slice_in_dim(value, half - mine, half)
        keep = lax.dynamic_slice_in_dim(value, mine, half)
        value = keep + swap(send, "wide", bit)
    for bit in reversed(bits):
        other = swap(value, "wide", bit)
        value = jnp.where(
            (where & bit) != 0,
            jnp.concatenate([other, value]),
            jnp.concatenate([value, other]),
        )
    return value


def call(kernel, name, outs, in_specs, out_specs, scratch, flops, moved, **more):
    return pl.pallas_call(
        kernel,
        name=name,
        out_shape=outs,
        in_specs=in_specs,
        out_specs=out_specs,
        scratch_shapes=scratch,
        cost_estimate=pl.CostEstimate(flops=flops, bytes_accessed=moved, transcendentals=0),
        compiler_params=pltpu.CompilerParams(vmem_limit_bytes=56 * MIB),
        **more,
    )


def dma(n):
    return pltpu.SemaphoreType.DMA((n,))


def per_device(
    images,
    labels,
    class_weight,
    basis_index,
    atom_mask,
    conv_weight,
    conv_momentum,
    batch_norm_params,
    norm_first,
    norm_second,
    head_weight,
    head_first,
    head_second,
    head_bias,
    bias_first,
    bias_second,
):
    count, width = images.shape[0], images.shape[3]
    local_rows = conv_weight.shape[1]
    rank = basis_index.shape[1]
    classes = head_weight.shape[0]
    devices = lax.axis_size("wide") * lax.axis_size("narrow")
    pixel_count = count * PIX * devices
    me_narrow = lax.axis_index("narrow")
    me = jnp.full((1,), me_narrow, jnp.int32)
    sds = jax.ShapeDtypeStruct
    field16 = sds((PIX, count, width), bf16)
    field32 = sds((PIX, count, width), f32)
    small = sds((8, width), f32)
    field_v16 = pltpu.VMEM((PIX, count, width), bf16)
    field_v32 = pltpu.VMEM((PIX, count, width), f32)
    weight_v = pltpu.VMEM((TAPS * width, width), bf16)
    conv_flops = 2 * 100 * count * width * width
    field_bytes = 4 * PIX * count * width

    low_weight = conv_weight.astype(bf16)

    def gather(layer):
        own = low_weight[layer]
        near = swap(own, "narrow", 1)
        far = swap(own, "narrow", 2)
        return own, near, far, swap(far, "narrow", 1)

    first_weight = gather(0)
    second_weight = gather(1)
    x = images.reshape(count, PIX, width).transpose(1, 0, 2)
    onehot = labels[:, None] == jnp.arange(classes, dtype=jnp.int32)[None, :]
    weight_sum = jnp.sum(jnp.where(onehot, class_weight.astype(f32)[None, :], 0.0))
    extra = jnp.full((1, width), weight_sum, f32)

    hid1, stats1 = call(
        conv_first_kernel,
        "conv_first",
        (field32, small),
        [SMEM, VMEM, ANY, ANY, ANY, ANY, ANY],
        (ANY, VMEM),
        [field_v16, weight_v, field_v32, dma(PIX), dma(4), dma(PIX)],
        conv_flops,
        2 * field_bytes,
    )(me, extra, x, *first_weight)
    stats1 = merge_moments(stats1, count * PIX)

    bases = cosine_rows(basis_index, width)
    basis_top = bases.astype(bf16)
    basis_rest = (bases - basis_top.astype(f32)).astype(bf16)
    basis_cat = jnp.concatenate([basis_top, basis_rest], axis=1).transpose(0, 2, 1)
    mask = atom_mask[:, 0].transpose(0, 2, 1).astype(f32)

    mom_gram = jnp.einsum(
        "lkc,lkd->lcd", conv_momentum, conv_momentum, precision=lax.Precision.HIGH
    )
    odd = (me_narrow & 1) != 0
    mine = jnp.where(odd, mom_gram[1], mom_gram[0])
    mine = mine + swap(jnp.where(odd, mom_gram[0], mom_gram[1]), "narrow", 1)
    mine = mine + swap(mine, "narrow", 2)
    other = swap(mine, "narrow", 1)
    mom_grams = (jnp.where(odd, other, mine), jnp.where(odd, mine, other))

    hid2, z1, stats2 = call(
        functools.partial(conv_second_kernel, pixel_count),
        "conv_second",
        (field32, field16, small),
        [SMEM, VMEM, VMEM, VMEM, ANY, ANY, ANY, ANY, ANY],
        (ANY, ANY, VMEM),
        [field_v32, field_v16, weight_v, field_v32, dma(PIX), dma(4), dma(PIX), dma(PIX)],
        conv_flops,
        3 * field_bytes,
    )(me, stats1[2:3], stats1, batch_norm_params, hid1, *second_weight)
    stats2 = merge_moments(stats2, count * PIX)
    weight_total = stats1[2, 0]

    head_low = jnp.pad(head_weight.astype(bf16), ((0, 128 - classes), (0, 0)))
    stats2 = jnp.concatenate([stats2[:2], stats1[2:3], stats2[3:]])
    slope2, dp, sums2, aux = call(
        functools.partial(head_kernel, pixel_count, classes),
        "head",
        (field32, sds((count, width), f32), small, sds((24, width), f32)),
        [VMEM, VMEM, VMEM, VMEM, VMEM, VMEM, ANY, ANY],
        (ANY, VMEM, VMEM, VMEM),
        [
            field_v32,
            field_v16,
            field_v32,
            pltpu.VMEM((count, width), bf16),
            pltpu.VMEM((count, width), f32),
            pltpu.VMEM((count, width), f32),
            dma(count // 32),
            dma(count // 32),
            dma(count // 32),
        ],
        conv_flops // 3,
        3 * field_bytes,
    )(
        stats2,
        batch_norm_params,
        head_low,
        jnp.pad(head_bias, (0, 128 - classes))[None],
        labels[:, None],
        jnp.pad(class_weight.astype(f32), (0, 128 - classes))[None],
        hid2,
        x,
    )
    sums2 = sum_all(sums2)
    aux = sum_all(aux)

    dh2, dy1, sums1 = call(
        functools.partial(second_grad_kernel, pixel_count),
        "second_grad",
        (field16, field32, small),
        [SMEM, VMEM, VMEM, VMEM, VMEM, VMEM] + [ANY] * 7,
        (ANY, ANY, VMEM),
        [
            field_v32,
            field_v32,
            field_v32,
            weight_v,
            field_v16,
            field_v32,
            dma(PIX),
            dma(PIX),
            dma(PIX),
            dma(4),
            dma(PIX),
            dma(PIX),
        ],
        conv_flops,
        5 * field_bytes,
    )(
        me,
        stats1,
        stats2,
        sums2,
        batch_norm_params,
        dp,
        hid2,
        slope2,
        hid1,
        *second_weight,
    )
    sums1 = sum_all(sums1)

    coef_outs = (sds((2, rank, local_rows), f32),) * 2
    coef_scratch = [
        pltpu.VMEM((PIX, 2 * rank, count), bf16),
        pltpu.VMEM((4, rank, local_rows), f32),
    ]
    keep2, send2 = call(
        coef_second_kernel,
        "coef_second",
        coef_outs,
        [SMEM, VMEM, ANY, ANY],
        (ANY, ANY),
        [field_v16, field_v16] + coef_scratch + [dma(PIX), dma(PIX), dma(4)],
        conv_flops // 2,
        2 * field_bytes,
    )(me, basis_cat[1], dh2, z1)

    def reduce_coef(keep, send, layer):
        other = swap(send, "narrow", 1)
        far = swap(keep[1] + other[1], "narrow", 2)
        return sum_wide((keep[0] + other[0] + far) * mask[layer])

    kept2 = reduce_coef(keep2, send2, 1)

    keep1, send1 = call(
        functools.partial(coef_first_kernel, pixel_count),
        "coef_first",
        coef_outs,
        [SMEM, VMEM, VMEM, VMEM, VMEM, ANY, ANY, ANY],
        (ANY, ANY),
        [field_v32, field_v32, field_v16] + coef_scratch + [dma(PIX), dma(PIX), dma(PIX), dma(4)],
        conv_flops // 2,
        3 * field_bytes,
    )(me, basis_cat[0], stats1, sums1, batch_norm_params, dy1, hid1, x)
    kept1 = reduce_coef(keep1, send1, 0)

    def ortho(kept, layer):
        parts = call(
            gram_parts_kernel,
            "gram_parts",
            sds((rank, width + rank), f32),
            [
                pl.BlockSpec((rank, local_rows), lambda i: (0, 0)),
                pl.BlockSpec((1, local_rows, width), lambda i: (layer, 0, 0)),
            ],
            pl.BlockSpec((rank, width + rank), lambda i: (0, 0)),
            [],
            6 * rank * local_rows * (width + rank),
            4 * local_rows * width,
            grid=(1,),
        )(kept, conv_momentum)
        parts = parts + swap(parts, "narrow", 1)
        parts = parts + swap(parts, "narrow", 2)
        return call(
            muon_kernel,
            "muon",
            (sds((width, width), f32), sds((8, 128), f32)),
            [VMEM] * 3,
            (VMEM, VMEM),
            [],
            6 * 17 * width**3,
            8 * width * width,
        )(mom_grams[layer], parts, bases[layer])

    step_rows = local_rows // 3

    def update(kept, layer, chain, scale, previous):
        rows = pl.BlockSpec((1, step_rows, width), lambda i: (layer, i, 0))
        whole = sds((2, local_rows, width), f32)
        return call(
            update_kernel,
            "update",
            (whole, whole, sds((2, local_rows, width), bf16)),
            [
                pl.BlockSpec((rank, step_rows), lambda i: (0, i)),
                pl.BlockSpec((rank, width), lambda i: (0, 0)),
                pl.BlockSpec((width, width), lambda i: (0, 0)),
                pl.BlockSpec((8, 128), lambda i: (0, 0)),
                rows,
                rows,
            ]
            + [ANY] * len(previous),
            (rows, rows, rows),
            [],
            6 * local_rows * width * width,
            20 * local_rows * width,
            grid=(local_rows // step_rows,),
            input_output_aliases={6 + i: i for i in range(len(previous))},
        )(kept, bases[layer], chain, scale, conv_momentum, conv_weight, *previous)

    chain2, scale2 = ortho(kept2, 1)
    outs = update(kept2, 1, chain2, scale2, ())
    chain1, scale1 = ortho(kept1, 0)
    new_weight, moment, low_copy = update(kept1, 0, chain1, scale1, outs)

    vector_grad = jnp.stack([sums1[1], sums1[0], sums2[1], sums2[0]])
    head_grad = aux[:classes]
    bias_grad = aux[16, :classes]
    loss_sum = aux[17, 0]
    vec, vec_m, vec_v = adamw(batch_norm_params, vector_grad, norm_first, norm_second, 0.3, 0.0)
    head_new, head_m, head_v = adamw(head_weight, head_grad, head_first, head_second, 0.03, 0.01)
    bias_new, bias_m, bias_v = adamw(head_bias, bias_grad, bias_first, bias_second, 0.3, 0.0)
    return (
        loss_sum,
        weight_total,
        new_weight,
        moment,
        low_copy,
        vec,
        vec_m,
        vec_v[:2],
        vec_v[2:],
        head_new,
        head_m,
        head_v,
        bias_new,
        bias_m,
        bias_v,
    )


def solution(mesh):
    rep = P()
    rows = P(None, "narrow", None)
    return jax.shard_map(
        per_device,
        mesh=mesh,
        in_specs=(
            P(("wide", "narrow"), None, None, None),
            P(("wide", "narrow")),
            rep,
            rep,
            P(None, "wide", "narrow", None),
            rows,
            rows,
        )
        + (rep,) * 9,
        out_specs=(rep, rep, rows, rows, rows) + (rep,) * 10,
        check_vma=False,
    )
```

```python
import functools

import jax
import jax.numpy as jnp
from jax import lax
from jax.experimental import pallas as pl
from jax.experimental.pallas import tpu as pltpu
from jax.sharding import PartitionSpec as P

SIDE = 4
PIX = SIDE * SIDE
TAPS = 9
NS_STEPS = 5
STEP = 5

f32 = jnp.float32
bf16 = jnp.bfloat16
highest = lax.Precision.HIGHEST
norm_eps = 1e-05
smooth = 0.1
ns_a, ns_b, ns_c = (3.4445, -4.775, 2.0315)
MIB = 1 << 20

ANY = pl.BlockSpec(memory_space=pl.ANY)
VMEM = pl.BlockSpec(memory_space=pltpu.VMEM)
SMEM = pl.BlockSpec(memory_space=pltpu.SMEM)


class Field:
    def __init__(self, refs):
        self.refs = refs

    def __getitem__(self, pixel):
        return self.refs[pixel // SIDE].at[pixel % SIDE]


def out_taps(pixel):
    p, q = divmod(pixel, SIDE)
    found = []
    for tap in range(TAPS):
        a, b = divmod(tap, 3)
        pp, qq = p + a - 1, q + b - 1
        if 0 <= pp < SIDE and 0 <= qq < SIDE:
            found.append((tap, pp * SIDE + qq))
    return found


def in_taps(pixel):
    found = []
    for out in range(PIX):
        for tap, source in out_taps(out):
            if source == pixel:
                found.append((tap, out))
    return found


def sigma_of(value):
    return 0.5 * jnp.tanh(0.5 * value) + 0.5


def weight_loads(me_ref, pieces, target, sems):
    me = me_ref[0]
    copies = []
    rows = pieces[0].shape[0]
    for k, piece in enumerate(pieces):
        start = pl.multiple_of((me ^ k) * rows, rows)
        copies.append(pltpu.make_async_copy(piece, target.at[pl.ds(start, rows)], sems.at[k]))
        copies[-1].start()
    return copies


def row_of(p):
    return list(range(p * SIDE, (p + 1) * SIDE)) if 0 <= p < SIDE else []


def cuts_of(count, size=32):
    return [slice(i, i + size) for i in range(0, count, size)]


def fold(value):
    return jnp.sum(value.reshape(-1, 8, value.shape[1]), axis=0)


def block_moments(block):
    cuts = cuts_of(block.shape[0])
    total = sum(fold(block[cut]) for cut in cuts)
    mean = jnp.sum(total, axis=0, keepdims=True) * (1.0 / block.shape[0])
    square = sum(fold(jnp.square(block[cut] - mean)) for cut in cuts)
    return mean, jnp.sum(square, axis=0, keepdims=True)


def store_moments(stats_ref, parts, rows, extra):
    mean = sum(m for m, _ in parts) * (1.0 / len(parts))
    square = sum(s for _, s in parts) + rows * sum(jnp.square(m - mean) for m, _ in parts)
    stats_ref[0:1] = mean
    stats_ref[1:2] = square
    stats_ref[2:3] = extra
    stats_ref[3:8] = jnp.zeros((5, mean.shape[1]), f32)


def conv_pixel(source, weight, pixel, width):
    total = None
    for tap, read in out_taps(pixel):
        part = jnp.dot(
            source[read][...], weight[tap * width : (tap + 1) * width], preferred_element_type=f32
        )
        total = part if total is None else total + part
    return total


def conv_first_kernel(me_ref, extra_ref, x_ref, w0, w1, w2, w3, h0, h1, h2, h3, stats_ref, w_v, ws):
    width = x_ref.shape[2]
    x_field, hid = Field([x_ref.at[pl.ds(p * SIDE, SIDE)] for p in range(SIDE)]), Field((h0, h1, h2, h3))
    for copy in weight_loads(me_ref, (w0, w1, w2, w3), w_v, ws):
        copy.wait()
    parts = []
    for pixel in range(PIX):
        hid[pixel][...] = conv_pixel(x_field, w_v, pixel, width)
        if pixel > 0:
            parts.append(block_moments(hid[pixel - 1]))
    parts.append(block_moments(hid[PIX - 1]))
    store_moments(stats_ref, parts, x_ref.shape[1], extra_ref[...])


def norm_rows(stats_ref, pixel_count):
    mean = stats_ref[0:1]
    return mean, lax.rsqrt(stats_ref[1:2] * (1.0 / pixel_count) + norm_eps)


def half_affine(scale, gain, shift):
    return 0.5 * (gain * scale), 0.5 * shift


def conv_second_kernel(pixel_count, me_ref, stats_in, params, *refs):
    h, weights, hid = Field(refs[:4]), refs[4:8], Field(refs[8:12])
    z_ref = refs[12]
    turned_refs = refs[13:16]
    stats_ref, w_v, ws = refs[16:]
    count, width = z_ref.shape[1:]
    z = Field([z_ref.at[pl.ds(p * SIDE, SIDE)] for p in range(SIDE)])
    wait_w = weight_loads(me_ref, weights, w_v, ws)
    mean, scale = norm_rows(stats_in, pixel_count)
    slope, offset = half_affine(scale, params[0:1], params[1:2])

    def activate(pixel):
        for cut in cuts_of(count):
            half = (h[pixel][cut] - mean) * slope + offset
            z[pixel][cut] = (half + half * jnp.tanh(half)).astype(bf16)

    first = SIDE + 2
    for pixel in range(first):
        activate(pixel)
    for copy in wait_w:
        copy.wait()
    parts = []
    for pixel in range(PIX):
        hid[pixel][...] = conv_pixel(z, w_v, pixel, width)
        if pixel + first < PIX:
            activate(pixel + first)
        if pixel < TAPS:
            turned_refs[pixel // 3][pixel % 3] = w_v[pixel * width : (pixel + 1) * width].T
        if pixel > 0:
            parts.append(block_moments(hid[pixel - 1]))
    parts.append(block_moments(hid[PIX - 1]))
    share = PIX * count / pixel_count
    store_moments(stats_ref, parts, count, stats_in[2:3] * share)


def head_kernel(
    pixel_count,
    classes,
    stats_in,
    params,
    head_ref,
    bias_ref,
    label_ref,
    class_ref,
    x_ref,
    *refs,
):
    h, slopes = Field(refs[:4]), Field(refs[4:8])
    dp_ref, sums_ref, aux_ref, pool_v, s1_v, s2_v = refs[8:]
    count, width = x_ref.shape[1:]
    rows = 32
    mean, scale = norm_rows(stats_in, pixel_count)
    slope_row, offset_row = half_affine(scale, params[2:3], params[3:4])

    def body(i, carry):
        here = pl.ds(pl.multiple_of(i * rows, rows), rows)
        for lane in range(0, width, 128):
            cut = slice(lane, lane + 128)
            slope, offset, middle = slope_row[:, cut], offset_row[:, cut], mean[:, cut]
            pool = jnp.zeros((rows, 128), f32)
            s1 = jnp.zeros((rows, 128), f32)
            s2 = jnp.zeros((rows, 128), f32)
            for pixel in range(PIX):
                hid = h[pixel][here, cut] - middle
                half = (hid * slope + offset) + 0.5 * x_ref[pixel, here, cut].astype(f32)
                turn = jnp.tanh(half)
                act = half + half * turn
                double = (1.0 + turn) + act * (1.0 - turn)
                slopes[pixel][here, cut] = double
                pool = pool + act
                s1 = s1 + double
                s2 = s2 + double * hid
            pool_v[here, cut] = (pool * (1.0 / PIX)).astype(bf16)
            s1_v[here, cut] = s1
            s2_v[here, cut] = s2
        return carry

    lax.fori_loop(0, count // rows, body, 0)
    pooled = pool_v[...]
    head = head_ref[...]
    logits = (
        lax.dot_general(pooled, head, (((1,), (1,)), ((), ())), preferred_element_type=f32)
        + bias_ref[...]
    )
    lane_index = lax.broadcasted_iota(jnp.int32, logits.shape, 1)
    valid = lane_index < classes
    label = jnp.broadcast_to(label_ref[...].astype(f32), logits.shape[::-1]).T
    onehot = (lane_index.astype(f32) == label).astype(f32)
    weight_each = jnp.sum(onehot * class_ref[...], axis=1, keepdims=True)
    top = jnp.max(jnp.where(valid, logits, -jnp.inf), axis=1, keepdims=True)
    moved = jnp.where(valid, logits - top, 0.0)
    powers = jnp.where(valid, jnp.exp(moved), 0.0)
    total = jnp.sum(powers, axis=1, keepdims=True)
    logp = jnp.where(valid, moved - jnp.log(total), 0.0)
    target = jnp.where(valid, (1.0 - smooth) * onehot + smooth / classes, 0.0)
    per_image = -jnp.sum(target * logp, axis=1, keepdims=True)
    loss = jnp.sum(weight_each * per_image, axis=0, keepdims=True)
    weight_total = stats_in[2:3, 0:1]
    dlogits = weight_each * (powers / total - target) / weight_total
    dp = (
        jnp.dot(dlogits, head.astype(f32), precision=highest, preferred_element_type=f32)
        * (0.5 / PIX)
    )
    dp_ref[...] = dp
    shift_sum = jnp.sum(dp * s1_v[...], axis=0, keepdims=True)
    raw_sum = jnp.sum(dp * s2_v[...], axis=0, keepdims=True)
    sums_ref[0:1] = shift_sum
    sums_ref[1:2] = raw_sum * scale
    sums_ref[2:8] = jnp.zeros((6, width), f32)
    head_grad = lax.dot_general(
        dlogits,
        pooled.astype(f32),
        (((0,), (0,)), ((), ())),
        precision=highest,
        preferred_element_type=f32,
    )
    aux_ref[0:16] = head_grad[0:16]
    aux_ref[16:24] = jnp.zeros((8, width), f32)
    aux_ref[16:17, 0:128] = jnp.sum(dlogits, axis=0, keepdims=True)
    aux_ref[17:18, 0:128] = jnp.broadcast_to(loss, (1, 128))


def second_grad_kernel(
    pixel_count,
    stats1,
    stats2,
    sums2,
    params,
    dp_ref,
    aux_ref,
    *refs,
):
    h2, slopes, h1, weights = Field(refs[:4]), Field(refs[4:8]), Field(refs[8:12]), refs[12:15]
    dh_ref, dy, sums_ref = refs[15], Field(refs[16:20]), refs[20]
    count, width = dh_ref.shape[1:]
    mean2, scale2 = norm_rows(stats2, pixel_count)
    outer = params[2:3] * scale2
    gain_part = -sums2[1:2] * (1.0 / pixel_count) * scale2 * outer
    shift_part = -sums2[0:1] * (1.0 / pixel_count) * outer - mean2 * gain_part
    mean1, scale1 = norm_rows(stats1, pixel_count)
    slope1, offset1 = half_affine(scale1, params[0:1], params[1:2])

    def hidden_grad(pixel):
        for cut in cuts_of(count):
            spread = (dp_ref[cut] * outer) * slopes[pixel][cut]
            dh_ref[pixel, cut] = (spread + (h2[pixel][cut] * gain_part + shift_part)).astype(bf16)

    def gather_grads(pixel):
        total = None
        for tap, out in in_taps(pixel):
            weight = weights[tap // 3][tap % 3]
            part = jnp.dot(dh_ref[out], weight, preferred_element_type=f32)
            total = part if total is None else total + part
        dy[pixel][...] = total

    def finish(pixel, shift_sum, raw_sum):
        for cut in cuts_of(count):
            hid = h1[pixel][cut] - mean1
            half = hid * slope1 + offset1
            turn = jnp.tanh(half)
            act = half + half * turn
            grad = dy[pixel][cut] * ((1.0 + turn) + act * (1.0 - turn))
            dy[pixel][cut] = grad
            shift_sum = shift_sum + fold(grad)
            raw_sum = raw_sum + fold(grad * hid)
        return shift_sum, raw_sum

    shift_sum = jnp.zeros((8, width), f32)
    raw_sum = jnp.zeros((8, width), f32)
    first = SIDE + 2
    for pixel in range(first):
        hidden_grad(pixel)
    for pixel in range(PIX):
        gather_grads(pixel)
        if pixel + first < PIX:
            hidden_grad(pixel + first)
        if pixel > 0:
            shift_sum, raw_sum = finish(pixel - 1, shift_sum, raw_sum)
    shift_sum, raw_sum = finish(PIX - 1, shift_sum, raw_sum)
    shift_sum = 0.5 * jnp.sum(shift_sum, axis=0, keepdims=True)
    raw_sum = 0.5 * jnp.sum(raw_sum, axis=0, keepdims=True)
    sums_ref[0:1] = shift_sum
    sums_ref[1:2] = raw_sum * scale1
    sums_ref[2:8] = jnp.zeros((6, width), f32)
    sums_ref[8:32] = aux_ref[...]


def coef_rows(spans, grad_of, source_ref, top_ref, rest_ref, basis_v, turned, add):
    rank = top_ref.shape[0]
    basis_v[:, :rank] = top_ref[...].T
    basis_v[:, rank:] = rest_ref[...].T

    def project(pixel):
        both = jnp.dot(grad_of(pixel), basis_v[...], preferred_element_type=f32)
        low = both[:, :rank] + both[:, rank:]
        top = low.astype(bf16)
        rest = (low - top.astype(f32)).astype(bf16)
        turned[pixel, :rank] = top.T
        turned[pixel, rank:] = rest.T

    for pixel in row_of(spans[0]):
        project(pixel)
    for p in spans:
        todo = row_of(p + 1) if p + 1 in spans else []
        for a in (1, 0, 2):
            if not 0 <= p + a - 1 < SIDE:
                continue
            for b in range(3):
                total = None
                for q in range(SIDE):
                    if 0 <= q + b - 1 < SIDE:
                        part = jnp.dot(
                            turned[p * SIDE + q],
                            source_ref[(p + a - 1) * SIDE + q + b - 1],
                            preferred_element_type=f32,
                        )
                        total = part if total is None else total + part
                add(p, 3 * a + b, total[:rank] + total[rank:])
                if todo:
                    project(todo.pop(0))


def store_coef(coef_v, mask_v, tap, coef):
    part_width = coef_v.shape[2]
    width = coef.shape[1]
    at = tap * width
    while at < (tap + 1) * width:
        j = at // part_width
        end = min((j + 1) * part_width, (tap + 1) * width)
        cut = slice(at - j * part_width, end - j * part_width)
        coef_v[j, :, cut] = (
            coef[:, at - tap * width : end - tap * width] * mask_v[j, :, cut].astype(f32)
        )
        at = end


PLANE = [(2 * (k & 1), k >> 1) for k in range(4)]
DEPTH = [(0, 2 * k) for k in range(4)]
NEAR, FAR = [(0, 0), (0, 2)], [(0, 0), (0, 4)]


def send_coef(me_ref, coef_v, keeps, send_any, sems, outer, inner):
    me, wide = me_ref[0], me_ref[1]
    rows = keeps[0].shape[1]
    copies = []
    for core in (1, 0):
        for i, (n0, w0) in enumerate(outer):
            for j, (n1, w1) in enumerate(inner):
                owner = wide ^ (w0 ^ w1)
                source = coef_v.at[
                    me ^ (core ^ n0 ^ n1), pl.ds(pl.multiple_of(owner * rows, rows), rows)
                ]
                target = send_any.at[i, j] if core else keeps[i].at[j]
                copies.append(pltpu.make_async_copy(source, target, sems.at[core]))
                copies[-1].start()
    for copy in copies:
        copy.wait()


def mask_loads(me_ref, pieces, target, sems):
    copies = [
        pltpu.make_async_copy(piece, target.at[me_ref[0] ^ k], sems.at[k])
        for k, piece in enumerate(pieces)
    ]
    for copy in copies:
        copy.start()
    return copies


def coef_top_kernel(top_ref, rest_ref, dh_ref, z_ref, sum_ref, basis_v, turned):
    seen = set()

    def add(p, tap, part):
        sum_ref[tap] = sum_ref[tap] + part if tap in seen else part
        seen.add(tap)

    coef_rows((0, 1), lambda i: dh_ref[i], z_ref, top_ref, rest_ref, basis_v, turned, add)


def coef_bottom_kernel(
    me_ref, top_ref, rest_ref, sum_ref, dh_ref, z_ref, *refs
):
    masks, keeps, refs = refs[:4], refs[4:6], refs[6:]
    send_any, basis_v, turned, sum_v, mask_v, coef_v, ms, sems = refs
    wait_mask = mask_loads(me_ref, masks, mask_v, ms)
    seen = set()

    def add(p, tap, part):
        if p == 3 and tap == 3:
            for copy in wait_mask:
                copy.wait()
        total = (sum_v if tap in seen else sum_ref)[tap] + part
        seen.add(tap)
        if p == 3:
            store_coef(coef_v, mask_v, tap, total)
        else:
            sum_v[tap] = total

    coef_rows((2, 3), lambda i: dh_ref[i], z_ref, top_ref, rest_ref, basis_v, turned, add)
    for tap in (6, 7, 8):
        store_coef(coef_v, mask_v, tap, sum_v[tap])
    inner = [(n, w ^ far) for n, w in PLANE for _, far in FAR]
    send_coef(me_ref, coef_v, keeps, send_any, sems, NEAR, inner)


def coef_first_kernel(
    pixel_count,
    me_ref,
    top_ref,
    rest_ref,
    stats1,
    sums1,
    params,
    x_ref,
    *refs,
):
    dy, h1, masks, keeps = Field(refs[:4]), Field(refs[4:8]), refs[8:12], refs[12:16]
    send_any, basis_v, turned, sum_v, mask_v, coef_v, ms, sems = refs[16:]
    wait_mask = mask_loads(me_ref, masks, mask_v, ms)
    mean, scale = norm_rows(stats1, pixel_count)
    outer = params[0:1] * scale
    gain_part = -sums1[1:2] * (1.0 / pixel_count) * scale * outer
    shift_part = -sums1[0:1] * (1.0 / pixel_count) * outer - mean * gain_part
    half_outer = 0.5 * outer
    seen = set()

    def grad_of(pixel):
        return jnp.concatenate(
            [
                (
                    dy[pixel][cut] * half_outer + (h1[pixel][cut] * gain_part + shift_part)
                ).astype(bf16)
                for cut in cuts_of(x_ref.shape[1])
            ],
            axis=0,
        )

    def add(p, tap, part):
        if p == 3 and tap == 3:
            for copy in wait_mask:
                copy.wait()
        total = sum_v[tap] + part if tap in seen else part
        seen.add(tap)
        if p == 3:
            store_coef(coef_v, mask_v, tap, total)
        else:
            sum_v[tap] = total

    coef_rows(range(SIDE), grad_of, x_ref, top_ref, rest_ref, basis_v, turned, add)
    for tap in (6, 7, 8):
        store_coef(coef_v, mask_v, tap, sum_v[tap])
    send_coef(me_ref, coef_v, keeps, send_any, sems, PLANE, DEPTH)


def add_parts_kernel(*refs):
    count = len(refs) // 2
    keeps, other, outs = refs[:count], refs[count], refs[count + 1 :]
    for part, (keep, out) in enumerate(zip(keeps, outs)):
        out[...] = keep[...] + other[part]


def add_pieces_kernel(received, *refs):
    parts, outs = refs[:received], refs[received:]
    size = parts[0].shape[0] // len(outs)
    for k, out in enumerate(outs):
        cut = pl.ds(k * size, size)
        total = tree([part[cut] for part in parts])
        out[...] = total.reshape(out.shape)


def halves(value):
    top = value.astype(bf16)
    return top, (value - top.astype(f32)).astype(bf16)


def dot3(left, right, dims=(((1,), (0,)), ((), ()))):
    (a, b), (c, d) = left, right

    def dot(x, y):
        return lax.dot_general(x, y, dims, preferred_element_type=f32)

    return dot(a, c) + (dot(a, d) + dot(b, c))


CONTRACT_ROWS = (((0,), (0,)), ((), ()))
CONTRACT_COLUMNS = (((1,), (1,)), ((), ()))


def piece_loads(me_ref, pieces, target, sems):
    rows = pieces[0].shape[0]
    copies = []
    for k, piece in enumerate(pieces):
        owner = me_ref[1] ^ k
        copies.append(
            pltpu.make_async_copy(
                piece, target.at[pl.ds(pl.multiple_of(owner * rows, rows), rows)], sems.at[k]
            )
        )
        copies[-1].start()
    return copies


def gram_parts_kernel(layer, pieces, me_ref, top_ref, rest_ref, mom_ref, *refs):
    kept_any, (out_ref, kept_v, ks) = refs[:pieces], refs[pieces:]
    for copy in piece_loads(me_ref, kept_any, kept_v, ks):
        copy.wait()
    rank = kept_v.shape[0]
    kept, rest = halves(kept_v[...])
    stacked = jnp.concatenate([kept, rest], axis=0)
    total, extra = None, None
    for cut in cuts_of(kept_v.shape[1], 384):
        top, low = halves(mom_ref[layer, cut])
        one = jnp.dot(stacked[:, cut], top, preferred_element_type=f32)
        two = jnp.dot(kept[:, cut], low, preferred_element_type=f32)
        total = one if total is None else total + one
        extra = two if extra is None else extra + two
    cross = total[:rank] + total[rank:] + extra
    square = dot3((kept, rest), (kept, rest), CONTRACT_COLUMNS)
    out_ref[...] = 0.95 * cross + 0.5 * dot3(halves(square), (top_ref[...], rest_ref[...]))


def moment_kernel(layer, pieces, me_ref, top_ref, rest_ref, mom_ref, *refs):
    kept_any, (new_ref, kept_v, ks) = refs[:pieces], refs[pieces:]
    for copy in piece_loads(me_ref, kept_any, kept_v, ks):
        copy.wait()
    kept = halves(kept_v[...])
    pair = (top_ref[...], rest_ref[...])
    for cut in cuts_of(kept_v.shape[1], 384):
        rebuilt = dot3((kept[0][:, cut], kept[1][:, cut]), pair, CONTRACT_ROWS)
        new_ref[cut] = 0.95 * mom_ref[layer, cut] + rebuilt


def pick_kernel(me_ref, a0, b0, a1, b1, out_ref):
    odd = (me_ref[0] & 1) == 1
    out_ref[...] = jnp.where(odd, a1[...] + b1[...], a0[...] + b0[...])


def chain_kernel(me_ref, gram_one, gram_two, one_ref, two_ref, top_ref, rest_ref, out_ref):
    layer = me_ref[0] & 1
    pair = (top_ref[layer], rest_ref[layer])
    side = dot3(halves(one_ref[...] + two_ref[...]), pair, CONTRACT_ROWS)
    gram = 0.9025 * (gram_one[...] + gram_two[...]) + (side + side.T)
    row = lax.broadcasted_iota(jnp.int32, gram.shape, 0)
    column = lax.broadcasted_iota(jnp.int32, gram.shape, 1)
    eye = (row == column).astype(f32)
    norm = jnp.sqrt(jnp.sum(gram * eye, keepdims=True)) + 1e-07
    inverse = 1.0 / norm
    gram = gram * (inverse * inverse)
    chain = None
    for step in range(NS_STEPS):
        gram_pair = halves(gram)
        poly = ns_b * gram + ns_c * dot3(gram_pair, gram_pair)
        poly_pair = halves(poly)
        if chain is None:
            chain = poly + ns_a * eye
        else:
            chain = ns_a * chain + dot3(halves(chain), poly_pair)
        if step + 1 < NS_STEPS:
            turn = ns_a * gram + dot3(gram_pair, poly_pair)
            gram = ns_a * turn + dot3(halves(turn), poly_pair)
    out_ref[...] = chain * (0.3 * inverse)


def update_kernel(apart, carried, me_ref, chain_ref, first_ref, second_ref, weight_ref, *refs):
    new_w, new_m, copy_any, fresh_v, low_v, os = refs[carried:]
    layer = (me_ref[0] & 1) ^ apart
    steps = os.shape[1]
    size = fresh_v.shape[0] // steps
    cuts = [pl.ds(i * size, size) for i in range(steps)]
    pair = halves(chain_ref[...])

    def send(source, target, sem, start=True):
        copy = pltpu.make_async_copy(source, target, sem)
        copy.start() if start else copy.wait()

    def moments(start):
        for k, ref in enumerate((first_ref, second_ref)):

            @pl.when(layer == k)
            def _():
                for i, cut in enumerate(cuts):
                    send(ref.at[cut], new_m.at[k, cut], os.at[0, i], start)

    moments(True)
    for i, cut in enumerate(cuts):
        moment = jnp.where(layer == 0, first_ref[cut], second_ref[cut])
        fresh = weight_ref[layer, cut] * (1.0 - 0.1 * 0.01) - dot3(halves(moment), pair)
        fresh_v[cut] = fresh
        low_v[cut] = fresh.astype(bf16)
        send(fresh_v.at[cut], new_w.at[layer, cut], os.at[1, i])
        send(low_v.at[cut], copy_any.at[layer, cut], os.at[2, i])
    moments(False)
    for i, cut in enumerate(cuts):
        send(fresh_v.at[cut], new_w.at[layer, cut], os.at[1, i], False)
        send(low_v.at[cut], copy_any.at[layer, cut], os.at[2, i], False)


def cosine_rows(index, width):
    cols = jnp.arange(width, dtype=f32)
    freq = index.astype(f32)[..., None]
    return jnp.sqrt(2.0 / width) * jnp.cos(jnp.pi * freq * (2.0 * cols + 1.0) / (2.0 * width))


def swap(value, narrow, wide=0):
    rows, columns = lax.axis_size("wide"), lax.axis_size("narrow")
    pairs = [
        (i * columns + j, (i ^ wide) * columns + (j ^ narrow))
        for i in range(rows)
        for j in range(columns)
    ]
    return lax.ppermute(value, ("wide", "narrow"), pairs)


def stages():
    bits = [(0, 1 << k) for k in range((lax.axis_size("wide") - 1).bit_length())]
    rest = [(2, 0)] + bits
    return [[(1, 0)]] + [rest[i : i + 2] for i in range(0, len(rest), 2)]


def partners(value, bits):
    found = [value]
    offsets = [(0, 0)]
    for narrow, wide in bits:
        offsets = offsets + [(n ^ narrow, w ^ wide) for n, w in offsets]
    for narrow, wide in offsets[1:]:
        found.append(swap(value, narrow, wide))
    return found


def tree(values):
    while len(values) > 1:
        values = [values[i] + values[i + 1] for i in range(0, len(values), 2)]
    return values[0]


def add_kernel(*refs):
    refs[-1][...] = tree([ref[...] for ref in refs[:-1]])


def add_up(parts):
    return call(
        add_kernel,
        "add",
        jax.ShapeDtypeStruct(parts[0].shape, parts[0].dtype),
        [VMEM] * len(parts),
        VMEM,
        [],
        parts[0].size,
        4 * parts[0].size,
        limit=2,
    )(*parts)


def sum_all(value, works=()):
    works = list(works)
    for bits in stages():
        value = add_up(partners(value, bits))
        if works:
            value, _ = lax.optimization_barrier((value, works.pop(0)()))
    return value


def moments_kernel(count, *refs):
    parts, out = [ref[...] for ref in refs[:-1]], refs[-1]
    mean = tree([part[0:1] for part in parts]) * (1.0 / len(parts))
    square = tree([part[1:2] for part in parts])
    apart = tree([jnp.square(part[0:1] - mean) for part in parts])
    out[0:1] = mean
    out[1:2] = square + count * apart
    out[2:3] = tree([part[2:3] for part in parts])
    out[3:8] = jnp.zeros((5, mean.shape[1]), f32)


def merge_moments(stats, count, works=()):
    works = list(works)
    for bits in stages():
        if works:
            stats = works.pop(0)(stats)
        parts = partners(stats, bits)
        stats = call(
            functools.partial(moments_kernel, count),
            "moments",
            jax.ShapeDtypeStruct(stats.shape, f32),
            [VMEM] * len(parts),
            VMEM,
            [],
            stats.size,
            4 * stats.size,
            limit=2,
        )(*parts)
        count = len(parts) * count
    return stats


def mom_gram_kernel(me_ref, mom_ref, keep_ref, send_ref):
    odd = me_ref[0] & 1
    for layer, out in ((odd, keep_ref), (1 - odd, send_ref)):
        pair = halves(mom_ref[layer])
        out[...] = dot3(pair, pair, CONTRACT_ROWS)


def adam_rows(param, grad, first, second, rate, decay):
    first = 0.9 * first + 0.1 * grad
    second = 0.999 * second + 0.001 * grad * grad
    mhat = first / (1.0 - 0.9**STEP)
    vhat = second / (1.0 - 0.999**STEP)
    return param - rate * (mhat / (jnp.sqrt(vhat) + 1e-08) + decay * param), first, second


def adam_kernel(
    s1, s2, vec, vec_m, vec_v, head, head_m, head_v, bias, bias_m, bias_v, *outs
):
    o_vec, o_vec_m, bottom, top, o_head, o_head_m, o_head_v, o_bias, o_bias_m, o_bias_v = outs
    rows = ((s1, 1, bottom), (s1, 0, bottom), (s2, 1, top), (s2, 0, top))
    for i, (sums, at, second) in enumerate(rows):
        new, first, square = adam_rows(
            vec[i : i + 1], sums[at : at + 1], vec_m[i : i + 1], vec_v[i : i + 1], 0.3, 0.0
        )
        o_vec[i : i + 1] = new
        o_vec_m[i : i + 1] = first
        second[i & 1 : (i & 1) + 1] = square
    classes = head.shape[0]
    o_head[...], o_head_m[...], o_head_v[...] = adam_rows(
        head[...], s1[8 : 8 + classes], head_m[...], head_v[...], 0.03, 0.01
    )
    o_bias[...], o_bias_m[...], o_bias_v[...] = adam_rows(
        bias[...], s1[24:25, 0:classes], bias_m[...], bias_v[...], 0.3, 0.0
    )


def call(kernel, name, outs, in_specs, out_specs, scratch, flops, moved, limit=10, **more):
    return pl.pallas_call(
        kernel,
        name=name,
        out_shape=outs,
        in_specs=in_specs,
        out_specs=out_specs,
        scratch_shapes=scratch,
        cost_estimate=pl.CostEstimate(flops=flops, bytes_accessed=moved, transcendentals=0),
        compiler_params=pltpu.CompilerParams(vmem_limit_bytes=limit * MIB),
        **more,
    )


def held(*values):
    return [pltpu.with_memory_space_constraint(value, pltpu.VMEM) for value in values]


def dma(n):
    return pltpu.SemaphoreType.DMA((n,))


def per_device(
    images,
    labels,
    class_weight,
    basis_index,
    atom_mask,
    conv_weight,
    conv_momentum,
    batch_norm_params,
    norm_first,
    norm_second,
    head_weight,
    head_first,
    head_second,
    head_bias,
    bias_first,
    bias_second,
):
    count, width = images.shape[0], images.shape[3]
    local_rows = conv_weight.shape[1]
    rank = basis_index.shape[1]
    classes = head_weight.shape[0]
    wides = lax.axis_size("wide")
    pixel_count = count * PIX * wides * lax.axis_size("narrow")
    me_narrow = lax.axis_index("narrow")
    low_wides = min(8, wides)
    me = jnp.stack([me_narrow, lax.axis_index("wide") & (low_wides - 1)]).astype(jnp.int32)
    sds = jax.ShapeDtypeStruct
    field16 = pltpu.VMEM((PIX, count, width), bf16)
    field32 = (pltpu.VMEM((SIDE, count, width), f32),) * SIDE
    small = sds((8, width), f32)
    weight_v = pltpu.VMEM((TAPS * width, width), bf16)
    conv_flops = 2 * 100 * count * width * width
    field_bytes = 4 * PIX * count * width

    low_weight = conv_weight.astype(bf16)

    def tie(*values):
        return lax.optimization_barrier(values)

    own = low_weight[0]
    near, far = swap(own, 1), swap(own, 2)
    x = images.reshape(count, PIX, width).transpose(1, 0, 2)
    onehot = labels[:, None] == jnp.arange(classes, dtype=jnp.int32)[None, :]
    weight_sum = jnp.sum(jnp.where(onehot, class_weight.astype(f32)[None, :], 0.0))
    extra = jnp.full((1, width), weight_sum, f32)
    bases = cosine_rows(basis_index, width)
    basis_top = bases.astype(bf16)
    basis_rest = (bases - basis_top.astype(f32)).astype(bf16)
    masks = atom_mask[:, 0].transpose(0, 2, 1).astype(bf16)
    head_low = jnp.pad(head_weight.astype(bf16), ((0, 128 - classes), (0, 0)))
    head_bias_row = jnp.pad(head_bias, (0, 128 - classes))[None]
    class_row = jnp.pad(class_weight.astype(f32), (0, 128 - classes))[None]
    prepared = (
        [low_weight[1], masks[0], masks[1]]
        + [basis_top[0], basis_top[1], basis_rest[0], basis_rest[1], basis_top, basis_rest]
        + [head_low, head_bias_row, class_row, labels[None]]
        + [row[None] for row in (head_bias, bias_first, bias_second)]
    )
    gram_keep, gram_send = call(
        mom_gram_kernel,
        "mom_gram",
        (sds((width, width), f32),) * 2,
        [SMEM, VMEM],
        (VMEM, VMEM),
        [],
        12 * local_rows * width * width,
        8 * local_rows * width,
        limit=16,
    )(me, conv_momentum)
    x, extra, me, far, prepared, gram_keep, gram_send = tie(
        x, extra, me, far, prepared, gram_keep, gram_send
    )
    first_weight = (own, near, far, swap(far, 1))
    gram_mine = add_up([gram_keep, swap(gram_send, 1)])
    second_own, mask0, mask1, top0, top1, rest0, rest1, bases_top, bases_rest = prepared[:9]
    head_low, head_bias_row, class_row, label_row, bias_row, bias_m_row, bias_v_row = prepared[9:]
    basis_top, basis_rest = (top0, top1), (rest0, rest1)
    second_near, second_far = swap(second_own, 1), swap(second_own, 2)

    *hid1, stats1 = call(
        conv_first_kernel,
        "conv_first",
        (*field32, small),
        [SMEM, VMEM, VMEM, ANY, ANY, ANY, ANY],
        (VMEM,) * 5,
        [weight_v, dma(4)],
        conv_flops,
        2 * field_bytes,
    )(me, extra, x, *first_weight)
    hid1 = held(*hid1)
    late = {}

    def last_weight(stats):
        stats, late["far"] = tie(stats, second_far)
        late["last"] = swap(late["far"], 1)
        return stats

    stats1 = merge_moments(stats1, count * PIX, (lambda s: s, lambda s: s, last_weight))

    stats1, gram_mine = tie(stats1, gram_mine)
    gram_other = swap(gram_mine, 2)
    second_weight = (second_own, second_near, late["far"], late["last"])

    outs = call(
        functools.partial(conv_second_kernel, pixel_count),
        "conv_second",
        (*field32, field16, *(pltpu.VMEM((3, width, width), bf16),) * 3, small),
        [SMEM] + [VMEM] * 6 + [ANY] * 4,
        (VMEM,) * 9,
        [weight_v, dma(4)],
        conv_flops,
        3 * field_bytes,
    )(me, stats1, batch_norm_params, *hid1, *second_weight)
    hid2, z1, turned_weight = held(*outs[:4]), held(outs[4])[0], held(*outs[5:8])
    stats2 = outs[8]
    stats2 = merge_moments(stats2, count * PIX)
    stats2, gram_other = tie(stats2, gram_other)

    *slope2, dp, sums2, aux = call(
        functools.partial(head_kernel, pixel_count, classes),
        "head",
        (*field32, sds((count, width), f32), small, sds((24, width), f32)),
        [VMEM] * 11,
        (VMEM,) * 7,
        [
            pltpu.VMEM((count, width), bf16),
            pltpu.VMEM((count, width), f32),
            pltpu.VMEM((count, width), f32),
        ],
        conv_flops // 3,
        3 * field_bytes,
    )(
        stats2,
        batch_norm_params,
        head_low,
        head_bias_row,
        label_row,
        class_row,
        x,
        *hid2,
    )
    slope2 = held(*slope2)
    sums2 = sum_all(sums2)
    sums2, mask0, mask1 = tie(sums2, mask0, mask1)
    gram_pair = (gram_mine, gram_other)
    mask_parts = [(mask, swap(mask, 1), swap(mask, 2)) for mask in (mask1, mask0)]

    dh2, *dy1, sums1 = call(
        functools.partial(second_grad_kernel, pixel_count),
        "second_grad",
        (field16, *field32, sds((32, width), f32)),
        [VMEM] * 21,
        (VMEM,) * 6,
        [],
        conv_flops,
        5 * field_bytes,
        input_output_aliases={10 + p: 1 + p for p in range(SIDE)},
    )(stats1, stats2, sums2, batch_norm_params, dp, aux, *hid2, *slope2, *hid1, *turned_weight)

    dh2, dy1 = held(dh2)[0], held(*dy1)
    sums1, far1, far0 = tie(sums1, mask_parts[0][2], mask_parts[1][2])
    masks = [
        (own, near, far, swap(far, 1))
        for (own, near, _), far in zip(mask_parts[::-1], (far0, far1))
    ]
    rows = rank // low_wides
    depth = low_wides // 2
    def coef_outs(outer):
        inner = 4 * depth // outer
        return (sds((inner, rows, local_rows), f32),) * outer + (
            sds((outer, inner, rows, local_rows), f32),
        )

    turned_v = pltpu.VMEM((PIX, 2 * rank, count), bf16)
    basis_v = pltpu.VMEM((width, 2 * rank), bf16)
    sum_v = pltpu.VMEM((TAPS, rank, width), f32)
    mask_v = pltpu.VMEM((4, rank, local_rows), bf16)
    coef_v = pltpu.VMEM((4, rank, local_rows), f32)
    results = {}

    def second_top():
        results["top"] = call(
            coef_top_kernel,
            "coef_top",
            sds((TAPS, rank, width), f32),
            [VMEM] * 4,
            VMEM,
            [basis_v, turned_v],
            conv_flops // 4,
            field_bytes,
        )(basis_top[1], basis_rest[1], dh2, z1)
        return results["top"]

    def second_bottom():
        results["second"] = call(
            coef_bottom_kernel,
            "coef_bottom",
            coef_outs(2),
            [SMEM] + [VMEM] * 5 + [ANY] * 4,
            (ANY,) * 3,
            [basis_v, turned_v, sum_v, mask_v, coef_v, dma(4), dma(2)],
            conv_flops // 4,
            field_bytes,
            limit=16,
        )(me, basis_top[1], basis_rest[1], results["top"], dh2, z1, *masks[1])
        return results["second"]

    def core_stage(outs):
        *keeps, send = outs
        return call(
            add_parts_kernel,
            "add_parts",
            [sds(keep.shape, f32) for keep in keeps],
            [VMEM] * (len(keeps) + 1),
            [VMEM] * len(keeps),
            [],
            rank * local_rows * 2,
            rank * local_rows * 24,
        )(*keeps, swap(send, 1))

    def reduce_stage(parts, offsets, cuts, after=()):
        received = [swap(part, *bits) for part, bits in zip(parts[1:], offsets[1:])]
        received, _ = tie(received, after)
        size = parts[0].shape[0] // cuts
        return call(
            functools.partial(add_pieces_kernel, len(parts)),
            "add_pieces",
            [sds((size, rows, local_rows), f32)] * cuts,
            [VMEM] * len(parts),
            [VMEM] * cuts,
            [],
            rank * local_rows,
            rank * local_rows * 12,
        )(parts[0], *received)

    def high_bits(own):
        own = own.reshape(rows, local_rows)
        bit = low_wides
        while bit < wides:
            own = add_up([own, swap(own, 0, bit)])
            bit = 2 * bit
        return own

    def spread(own):
        found = {0: own}
        for z in range(1, depth):
            found[2 * z] = swap(own, 0, 2 * z)
        found[1] = swap(own, 0, 1)
        for z in range(1, depth):
            found[2 * z + 1] = swap(found[2 * z], 0, 1)
        return [found[k] for k in range(low_wides)]

    def gram_stage(pieces, layer):
        parts = call(
            functools.partial(gram_parts_kernel, layer, low_wides),
            "gram_parts",
            sds((rank, width), f32),
            [SMEM, VMEM, VMEM, VMEM] + [ANY] * low_wides,
            VMEM,
            [pltpu.VMEM((rank, local_rows), f32), dma(low_wides)],
            6 * rank * local_rows * (width + rank),
            4 * local_rows * width,
        )(me, basis_top[layer], basis_rest[layer], conv_momentum, *pieces)
        return parts, swap(parts, 1)

    whole = sds((2, local_rows, width), f32)
    block_v = pltpu.VMEM((local_rows, width), f32)

    def moment_stage(pieces, layer):
        return call(
            functools.partial(moment_kernel, layer, low_wides),
            "moment",
            sds((local_rows, width), f32),
            [SMEM, VMEM, VMEM, VMEM] + [ANY] * low_wides,
            VMEM,
            [pltpu.VMEM((rank, local_rows), f32), dma(low_wides)],
            6 * local_rows * width * rank,
            8 * local_rows * width,
        )(me, basis_top[layer], basis_rest[layer], conv_momentum, *pieces)

    def update_stage(apart, chain, previous):
        carried = len(previous)
        return call(
            functools.partial(update_kernel, apart, carried),
            "update",
            (whole, whole, sds((2, local_rows, width), bf16)),
            [SMEM] + [VMEM] * 4 + [ANY] * carried,
            (ANY,) * 3,
            [block_v, pltpu.VMEM((local_rows, width), bf16), pltpu.SemaphoreType.DMA((3, 3))],
            6 * local_rows * width * width,
            16 * local_rows * width,
            limit=16,
            input_output_aliases={5 + i: i for i in range(carried)},
        )(me, chain, moment1, moment2, conv_weight, *previous)

    def second_core():
        results["parts"] = core_stage(results["second"])
        return results["parts"]

    sums1 = sum_all(sums1, (second_top, second_bottom, second_core))
    first = call(
        functools.partial(coef_first_kernel, pixel_count),
        "coef_first",
        coef_outs(4),
        [SMEM] + [VMEM] * 14 + [ANY] * 4,
        (ANY,) * 5,
        [basis_v, turned_v, sum_v, mask_v, coef_v, dma(4), dma(2)],
        conv_flops // 2,
        3 * field_bytes,
        limit=16,
    )(me, basis_top[0], basis_rest[0], stats1, sums1, batch_norm_params, x, *dy1, *hid1, *masks[0])

    parts1 = core_stage(first)
    parts2 = results["parts"]
    pieces1 = reduce_stage(parts1, PLANE, 4)
    pieces2 = reduce_stage(parts2, NEAR, 4, pieces1)
    (own1,) = reduce_stage(pieces1, DEPTH, 1)
    halves2 = reduce_stage(pieces2, PLANE, 2)
    own1 = high_bits(own1)
    all1 = spread(own1)
    (own2,) = reduce_stage(halves2, FAR, 1, own1)
    own2 = high_bits(own2)
    all2 = spread(own2)
    grams2 = gram_stage(all2, 1)
    moment2 = moment_stage(all2, 1)
    all1[0], moment2 = tie(all1[0], moment2)
    grams1 = gram_stage(all1, 0)
    mine = call(
        pick_kernel,
        "pick",
        sds((rank, width), f32),
        [SMEM] + [VMEM] * 4,
        VMEM,
        [],
        rank * width,
        20 * rank * width,
        limit=4,
    )(me, *grams1, *grams2)
    other = swap(mine, 2)
    moment1 = moment_stage(all1, 0)
    other, moment1 = tie(other, moment1)
    chain = call(
        chain_kernel,
        "chain",
        sds((width, width), f32),
        [SMEM] + [VMEM] * 6,
        VMEM,
        [],
        6 * 17 * width**3,
        8 * width * width,
        limit=24,
    )(me, *gram_pair, mine, other, bases_top, bases_rest)
    far_chain = swap(chain, 1)
    outs = update_stage(0, chain, ())
    new_weight, moment, low_copy = update_stage(1, far_chain, outs)

    row, pair, column = sds((4, width), f32), sds((2, width), f32), sds((classes, width), f32)
    line = sds((1, classes), f32)
    vec, vec_m, bottom, top, head_new, head_m, head_v, bias_new, bias_m, bias_v = call(
        adam_kernel,
        "adam",
        (row, row, pair, pair, column, column, column, line, line, line),
        [VMEM] * 11,
        (VMEM,) * 10,
        [],
        100 * classes * width,
        40 * classes * width,
        limit=2,
    )(
        sums1,
        sums2,
        batch_norm_params,
        norm_first,
        norm_second,
        head_weight,
        head_first,
        head_second,
        bias_row,
        bias_m_row,
        bias_v_row,
    )
    return (
        sums1[25, 0],
        stats1[2, 0],
        new_weight,
        moment,
        low_copy,
        vec,
        vec_m,
        bottom,
        top,
        head_new,
        head_m,
        head_v,
        bias_new[0],
        bias_m[0],
        bias_v[0],
    )


def solution(mesh):
    rep = P()
    rows = P(None, "narrow", None)
    return jax.shard_map(
        per_device,
        mesh=mesh,
        in_specs=(
            P(("wide", "narrow"), None, None, None),
            P(("wide", "narrow")),
            rep,
            rep,
            P(None, "wide", "narrow", None),
            rows,
            rows,
        )
        + (rep,) * 9,
        out_specs=(rep, rep, rows, rows, rows) + (rep,) * 10,
        check_vma=False,
    )
```

```python
import functools

import jax
import jax.numpy as jnp
from jax import lax
from jax.experimental import pallas as pl
from jax.experimental.pallas import tpu as pltpu
from jax.sharding import PartitionSpec as P

SIDE = 4
PIX = SIDE * SIDE
TAPS = 9
NS_STEPS = 5
STEP = 5

f32 = jnp.float32
bf16 = jnp.bfloat16
highest = lax.Precision.HIGHEST
norm_eps = 1e-05
smooth = 0.1
ns_a, ns_b, ns_c = (3.4445, -4.775, 2.0315)
MIB = 1 << 20

ANY = pl.BlockSpec(memory_space=pl.ANY)
VMEM = pl.BlockSpec(memory_space=pltpu.VMEM)
SMEM = pl.BlockSpec(memory_space=pltpu.SMEM)


class Field:
    def __init__(self, refs):
        self.refs = refs

    def __getitem__(self, pixel):
        return self.refs[pixel // SIDE].at[pixel % SIDE]


def out_taps(pixel):
    p, q = divmod(pixel, SIDE)
    found = []
    for tap in range(TAPS):
        a, b = divmod(tap, 3)
        pp, qq = p + a - 1, q + b - 1
        if 0 <= pp < SIDE and 0 <= qq < SIDE:
            found.append((tap, pp * SIDE + qq))
    return found


def in_taps(pixel):
    found = []
    for out in range(PIX):
        for tap, source in out_taps(out):
            if source == pixel:
                found.append((tap, out))
    return found


def sigma_of(value):
    return 0.5 * jnp.tanh(0.5 * value) + 0.5


def weight_loads(me_ref, pieces, target, sems):
    me = me_ref[0]
    copies = []
    rows = pieces[0].shape[0]
    for k, piece in enumerate(pieces):
        start = pl.multiple_of((me ^ k) * rows, rows)
        copies.append(pltpu.make_async_copy(piece, target.at[pl.ds(start, rows)], sems.at[k]))
        copies[-1].start()
    return copies


def row_of(p):
    return list(range(p * SIDE, (p + 1) * SIDE)) if 0 <= p < SIDE else []


def cuts_of(count, size=32):
    return [slice(i, i + size) for i in range(0, count, size)]


def fold(value):
    return jnp.sum(value.reshape(-1, 8, value.shape[1]), axis=0)


def block_moments(block):
    cuts = cuts_of(block.shape[0])
    total = sum(fold(block[cut]) for cut in cuts)
    mean = jnp.sum(total, axis=0, keepdims=True) * (1.0 / block.shape[0])
    square = sum(fold(jnp.square(block[cut] - mean)) for cut in cuts)
    return mean, jnp.sum(square, axis=0, keepdims=True)


def store_moments(stats_ref, parts, rows, extra):
    mean = sum(m for m, _ in parts) * (1.0 / len(parts))
    square = sum(s for _, s in parts) + rows * sum(jnp.square(m - mean) for m, _ in parts)
    stats_ref[0:1] = mean
    stats_ref[1:2] = square
    stats_ref[2:3] = extra
    stats_ref[3:8] = jnp.zeros((5, mean.shape[1]), f32)


def conv_pixel(source, weight, pixel, width):
    total = None
    for tap, read in out_taps(pixel):
        part = jnp.dot(
            source[read][...], weight[tap * width : (tap + 1) * width], preferred_element_type=f32
        )
        total = part if total is None else total + part
    return total


def conv_first_kernel(me_ref, extra_ref, x_ref, w0, w1, w2, w3, h0, h1, h2, h3, stats_ref, w_v, ws):
    width = x_ref.shape[2]
    x_field, hid = Field([x_ref.at[pl.ds(p * SIDE, SIDE)] for p in range(SIDE)]), Field((h0, h1, h2, h3))
    for copy in weight_loads(me_ref, (w0, w1, w2, w3), w_v, ws):
        copy.wait()
    parts = []
    for pixel in range(PIX):
        hid[pixel][...] = conv_pixel(x_field, w_v, pixel, width)
        if pixel > 0:
            parts.append(block_moments(hid[pixel - 1]))
    parts.append(block_moments(hid[PIX - 1]))
    store_moments(stats_ref, parts, x_ref.shape[1], extra_ref[...])


def norm_rows(stats_ref, pixel_count):
    mean = stats_ref[0:1]
    return mean, lax.rsqrt(stats_ref[1:2] * (1.0 / pixel_count) + norm_eps)


def half_affine(scale, gain, shift):
    return 0.5 * (gain * scale), 0.5 * shift


def conv_second_kernel(pixel_count, me_ref, stats_in, params, *refs):
    h, weights, hid = Field(refs[:4]), refs[4:8], Field(refs[8:12])
    z_ref = refs[12]
    turned_refs = refs[13:16]
    stats_ref, w_v, ws = refs[16:]
    count, width = z_ref.shape[1:]
    z = Field([z_ref.at[pl.ds(p * SIDE, SIDE)] for p in range(SIDE)])
    wait_w = weight_loads(me_ref, weights, w_v, ws)
    mean, scale = norm_rows(stats_in, pixel_count)
    slope, offset = half_affine(scale, params[0:1], params[1:2])

    def activate(pixel):
        for cut in cuts_of(count):
            half = (h[pixel][cut] - mean) * slope + offset
            z[pixel][cut] = (half + half * jnp.tanh(half)).astype(bf16)

    first = SIDE + 2
    for pixel in range(first):
        activate(pixel)
    for copy in wait_w:
        copy.wait()
    parts = []
    for pixel in range(PIX):
        hid[pixel][...] = conv_pixel(z, w_v, pixel, width)
        if pixel + first < PIX:
            activate(pixel + first)
        if pixel < TAPS:
            turned_refs[pixel // 3][pixel % 3] = w_v[pixel * width : (pixel + 1) * width].T
        if pixel > 0:
            parts.append(block_moments(hid[pixel - 1]))
    parts.append(block_moments(hid[PIX - 1]))
    share = PIX * count / pixel_count
    store_moments(stats_ref, parts, count, stats_in[2:3] * share)


def head_kernel(
    pixel_count,
    classes,
    stats_in,
    params,
    head_ref,
    bias_ref,
    label_ref,
    class_ref,
    x_ref,
    *refs,
):
    h, slopes = Field(refs[:4]), Field(refs[4:8])
    dp_ref, sums_ref, aux_ref, pool_v, s1_v, s2_v = refs[8:]
    count, width = x_ref.shape[1:]
    rows = 32
    mean, scale = norm_rows(stats_in, pixel_count)
    slope_row, offset_row = half_affine(scale, params[2:3], params[3:4])

    def body(i, carry):
        here = pl.ds(pl.multiple_of(i * rows, rows), rows)
        for lane in range(0, width, 128):
            cut = slice(lane, lane + 128)
            slope, offset, middle = slope_row[:, cut], offset_row[:, cut], mean[:, cut]
            pool = jnp.zeros((rows, 128), f32)
            s1 = jnp.zeros((rows, 128), f32)
            s2 = jnp.zeros((rows, 128), f32)
            for pixel in range(PIX):
                hid = h[pixel][here, cut] - middle
                half = (hid * slope + offset) + 0.5 * x_ref[pixel, here, cut].astype(f32)
                turn = jnp.tanh(half)
                act = half + half * turn
                double = (1.0 + turn) + act * (1.0 - turn)
                slopes[pixel][here, cut] = double
                pool = pool + act
                s1 = s1 + double
                s2 = s2 + double * hid
            pool_v[here, cut] = (pool * (1.0 / PIX)).astype(bf16)
            s1_v[here, cut] = s1
            s2_v[here, cut] = s2
        return carry

    lax.fori_loop(0, count // rows, body, 0)
    pooled = pool_v[...]
    head = head_ref[...]
    logits = (
        lax.dot_general(pooled, head, (((1,), (1,)), ((), ())), preferred_element_type=f32)
        + bias_ref[...]
    )
    lane_index = lax.broadcasted_iota(jnp.int32, logits.shape, 1)
    valid = lane_index < classes
    label = jnp.broadcast_to(label_ref[...].astype(f32), logits.shape[::-1]).T
    onehot = (lane_index.astype(f32) == label).astype(f32)
    weight_each = jnp.sum(onehot * class_ref[...], axis=1, keepdims=True)
    top = jnp.max(jnp.where(valid, logits, -jnp.inf), axis=1, keepdims=True)
    moved = jnp.where(valid, logits - top, 0.0)
    powers = jnp.where(valid, jnp.exp(moved), 0.0)
    total = jnp.sum(powers, axis=1, keepdims=True)
    logp = jnp.where(valid, moved - jnp.log(total), 0.0)
    target = jnp.where(valid, (1.0 - smooth) * onehot + smooth / classes, 0.0)
    per_image = -jnp.sum(target * logp, axis=1, keepdims=True)
    loss = jnp.sum(weight_each * per_image, axis=0, keepdims=True)
    weight_total = stats_in[2:3, 0:1]
    dlogits = weight_each * (powers / total - target) / weight_total
    dp = (
        jnp.dot(dlogits, head.astype(f32), precision=highest, preferred_element_type=f32)
        * (0.5 / PIX)
    )
    dp_ref[...] = dp
    shift_sum = jnp.sum(dp * s1_v[...], axis=0, keepdims=True)
    raw_sum = jnp.sum(dp * s2_v[...], axis=0, keepdims=True)
    sums_ref[0:1] = shift_sum
    sums_ref[1:2] = raw_sum * scale
    sums_ref[2:8] = jnp.zeros((6, width), f32)
    head_grad = lax.dot_general(
        dlogits,
        pooled.astype(f32),
        (((0,), (0,)), ((), ())),
        precision=highest,
        preferred_element_type=f32,
    )
    aux_ref[0:16] = head_grad[0:16]
    aux_ref[16:24] = jnp.zeros((8, width), f32)
    aux_ref[16:17, 0:128] = jnp.sum(dlogits, axis=0, keepdims=True)
    aux_ref[17:18, 0:128] = jnp.broadcast_to(loss, (1, 128))


def second_grad_kernel(
    pixel_count,
    stats1,
    stats2,
    sums2,
    params,
    dp_ref,
    aux_ref,
    *refs,
):
    h2, slopes, h1, weights = Field(refs[:4]), Field(refs[4:8]), Field(refs[8:12]), refs[12:15]
    dh_ref, dy, sums_ref = refs[15], Field(refs[16:20]), refs[20]
    count, width = dh_ref.shape[1:]
    mean2, scale2 = norm_rows(stats2, pixel_count)
    outer = params[2:3] * scale2
    gain_part = -sums2[1:2] * (1.0 / pixel_count) * scale2 * outer
    shift_part = -sums2[0:1] * (1.0 / pixel_count) * outer
    mean1, scale1 = norm_rows(stats1, pixel_count)
    slope1, offset1 = half_affine(scale1, params[0:1], params[1:2])

    def hidden_grad(pixel):
        for cut in cuts_of(count):
            spread = (dp_ref[cut] * outer) * slopes[pixel][cut]
            dh_ref[pixel, cut] = (spread + ((h2[pixel][cut] - mean2) * gain_part + shift_part)).astype(bf16)

    def gather_grads(pixel):
        total = None
        for tap, out in in_taps(pixel):
            weight = weights[tap // 3][tap % 3]
            part = jnp.dot(dh_ref[out], weight, preferred_element_type=f32)
            total = part if total is None else total + part
        dy[pixel][...] = total

    def finish(pixel, shift_sum, raw_sum):
        for cut in cuts_of(count):
            hid = h1[pixel][cut] - mean1
            half = hid * slope1 + offset1
            turn = jnp.tanh(half)
            act = half + half * turn
            grad = dy[pixel][cut] * ((1.0 + turn) + act * (1.0 - turn))
            dy[pixel][cut] = grad
            shift_sum = shift_sum + fold(grad)
            raw_sum = raw_sum + fold(grad * hid)
        return shift_sum, raw_sum

    shift_sum = jnp.zeros((8, width), f32)
    raw_sum = jnp.zeros((8, width), f32)
    first = SIDE + 2
    for pixel in range(first):
        hidden_grad(pixel)
    for pixel in range(PIX):
        gather_grads(pixel)
        if pixel + first < PIX:
            hidden_grad(pixel + first)
        if pixel > 0:
            shift_sum, raw_sum = finish(pixel - 1, shift_sum, raw_sum)
    shift_sum, raw_sum = finish(PIX - 1, shift_sum, raw_sum)
    shift_sum = 0.5 * jnp.sum(shift_sum, axis=0, keepdims=True)
    raw_sum = 0.5 * jnp.sum(raw_sum, axis=0, keepdims=True)
    sums_ref[0:1] = shift_sum
    sums_ref[1:2] = raw_sum * scale1
    sums_ref[2:8] = jnp.zeros((6, width), f32)
    sums_ref[8:32] = aux_ref[...]


def coef_rows(spans, grad_of, source_ref, top_ref, rest_ref, basis_v, turned, add):
    rank = top_ref.shape[0]
    basis_v[:, :rank] = top_ref[...].T
    basis_v[:, rank:] = rest_ref[...].T

    def project(pixel):
        both = jnp.dot(grad_of(pixel), basis_v[...], preferred_element_type=f32)
        low = both[:, :rank] + both[:, rank:]
        top = low.astype(bf16)
        rest = (low - top.astype(f32)).astype(bf16)
        turned[pixel, :rank] = top.T
        turned[pixel, rank:] = rest.T

    for pixel in row_of(spans[0]):
        project(pixel)
    for p in spans:
        todo = row_of(p + 1) if p + 1 in spans else []
        for a in (1, 0, 2):
            if not 0 <= p + a - 1 < SIDE:
                continue
            for b in range(3):
                total = None
                for q in range(SIDE):
                    if 0 <= q + b - 1 < SIDE:
                        part = jnp.dot(
                            turned[p * SIDE + q],
                            source_ref[(p + a - 1) * SIDE + q + b - 1],
                            preferred_element_type=f32,
                        )
                        total = part if total is None else total + part
                add(p, 3 * a + b, total[:rank] + total[rank:])
                if todo:
                    project(todo.pop(0))


def store_coef(coef_v, mask_v, tap, coef):
    part_width = coef_v.shape[2]
    width = coef.shape[1]
    at = tap * width
    while at < (tap + 1) * width:
        j = at // part_width
        end = min((j + 1) * part_width, (tap + 1) * width)
        cut = slice(at - j * part_width, end - j * part_width)
        coef_v[j, :, cut] = (
            coef[:, at - tap * width : end - tap * width] * mask_v[j, :, cut].astype(f32)
        )
        at = end


PLANE = [(2 * (k & 1), k >> 1) for k in range(4)]
DEPTH = [(0, 2 * k) for k in range(4)]
NEAR, FAR = [(0, 0), (0, 2)], [(0, 0), (0, 4)]


def send_coef(me_ref, coef_v, keeps, send_ref, outer, inner):
    me, wide = me_ref[0], me_ref[1]
    rows = keeps[0].shape[1]
    for core in (1, 0):
        for i, (n0, w0) in enumerate(outer):
            for j, (n1, w1) in enumerate(inner):
                start = pl.multiple_of((wide ^ (w0 ^ w1)) * rows, rows)
                piece = coef_v[me ^ (core ^ n0 ^ n1), pl.ds(start, rows)]
                if core:
                    send_ref[i, j] = piece
                else:
                    keeps[i][j] = piece


def mask_loads(me_ref, pieces, target, sems):
    copies = [
        pltpu.make_async_copy(piece, target.at[me_ref[0] ^ k], sems.at[k])
        for k, piece in enumerate(pieces)
    ]
    for copy in copies:
        copy.start()
    return copies


def coef_top_kernel(top_ref, rest_ref, dh_ref, z_ref, sum_ref, basis_v, turned):
    seen = set()

    def add(p, tap, part):
        sum_ref[tap] = sum_ref[tap] + part if tap in seen else part
        seen.add(tap)

    coef_rows((0, 1), lambda i: dh_ref[i], z_ref, top_ref, rest_ref, basis_v, turned, add)


def coef_bottom_kernel(
    me_ref, top_ref, rest_ref, sum_ref, dh_ref, z_ref, *refs
):
    masks, keeps, refs = refs[:4], refs[4:6], refs[6:]
    send_ref, basis_v, turned, sum_v, mask_v, coef_v, ms = refs
    wait_mask = mask_loads(me_ref, masks, mask_v, ms)
    seen = set()

    def add(p, tap, part):
        if p == 3 and tap == 3:
            for copy in wait_mask:
                copy.wait()
        total = (sum_v if tap in seen else sum_ref)[tap] + part
        seen.add(tap)
        if p == 3:
            store_coef(coef_v, mask_v, tap, total)
        else:
            sum_v[tap] = total

    coef_rows((2, 3), lambda i: dh_ref[i], z_ref, top_ref, rest_ref, basis_v, turned, add)
    for tap in (6, 7, 8):
        store_coef(coef_v, mask_v, tap, sum_v[tap])
    inner = [(n, w ^ far) for n, w in PLANE for _, far in FAR]
    send_coef(me_ref, coef_v, keeps, send_ref, NEAR, inner)


def coef_first_kernel(
    pixel_count,
    me_ref,
    top_ref,
    rest_ref,
    stats1,
    sums1,
    params,
    x_ref,
    *refs,
):
    dy, h1, masks, keeps = Field(refs[:4]), Field(refs[4:8]), refs[8:12], refs[12:16]
    send_ref, basis_v, turned, sum_v, mask_v, coef_v, ms = refs[16:]
    wait_mask = mask_loads(me_ref, masks, mask_v, ms)
    mean, scale = norm_rows(stats1, pixel_count)
    outer = params[0:1] * scale
    gain_part = -sums1[1:2] * (1.0 / pixel_count) * scale * outer
    shift_part = -sums1[0:1] * (1.0 / pixel_count) * outer
    half_outer = 0.5 * outer
    seen = set()

    def grad_of(pixel):
        return jnp.concatenate(
            [
                (
                    dy[pixel][cut] * half_outer
                    + ((h1[pixel][cut] - mean) * gain_part + shift_part)
                ).astype(bf16)
                for cut in cuts_of(x_ref.shape[1])
            ],
            axis=0,
        )

    def add(p, tap, part):
        if p == 3 and tap == 3:
            for copy in wait_mask:
                copy.wait()
        total = sum_v[tap] + part if tap in seen else part
        seen.add(tap)
        if p == 3:
            store_coef(coef_v, mask_v, tap, total)
        else:
            sum_v[tap] = total

    coef_rows(range(SIDE), grad_of, x_ref, top_ref, rest_ref, basis_v, turned, add)
    for tap in (6, 7, 8):
        store_coef(coef_v, mask_v, tap, sum_v[tap])
    send_coef(me_ref, coef_v, keeps, send_ref, PLANE, DEPTH)


def add_parts_kernel(*refs):
    count = len(refs) // 2
    keeps, other, outs = refs[:count], refs[count], refs[count + 1 :]
    for part, (keep, out) in enumerate(zip(keeps, outs)):
        out[...] = keep[...] + other[part]


def add_pieces_kernel(received, *refs):
    parts, outs = refs[:received], refs[received:]
    size = parts[0].shape[0] // len(outs)
    for k, out in enumerate(outs):
        cut = pl.ds(k * size, size)
        total = tree([part[cut] for part in parts])
        out[...] = total.reshape(out.shape)


def halves(value):
    top = value.astype(bf16)
    return top, (value - top.astype(f32)).astype(bf16)


def dot3(left, right, dims=(((1,), (0,)), ((), ()))):
    (a, b), (c, d) = left, right

    def dot(x, y):
        return lax.dot_general(x, y, dims, preferred_element_type=f32)

    return dot(a, c) + (dot(a, d) + dot(b, c))


CONTRACT_ROWS = (((0,), (0,)), ((), ()))
CONTRACT_COLUMNS = (((1,), (1,)), ((), ()))


def gather_pieces(me_ref, pieces, target):
    rows = pieces[0].shape[0]
    for k, piece in enumerate(pieces):
        start = pl.multiple_of((me_ref[1] ^ k) * rows, rows)
        target[pl.ds(start, rows)] = piece[...]


def gram_parts_kernel(layer, pieces, me_ref, top_ref, rest_ref, mom_ref, *refs):
    out_ref, kept_v = refs[pieces:]
    gather_pieces(me_ref, refs[:pieces], kept_v)
    rank = kept_v.shape[0]
    kept, rest = halves(kept_v[...])
    stacked = jnp.concatenate([kept, rest], axis=0)
    total, extra = None, None
    for cut in cuts_of(kept_v.shape[1], 384):
        top, low = halves(mom_ref[layer, cut])
        one = jnp.dot(stacked[:, cut], top, preferred_element_type=f32)
        two = jnp.dot(kept[:, cut], low, preferred_element_type=f32)
        total = one if total is None else total + one
        extra = two if extra is None else extra + two
    cross = total[:rank] + total[rank:] + extra
    square = dot3((kept, rest), (kept, rest), CONTRACT_COLUMNS)
    out_ref[...] = 0.95 * cross + 0.5 * dot3(halves(square), (top_ref[...], rest_ref[...]))


def moment_kernel(layer, pieces, me_ref, top_ref, rest_ref, mom_ref, *refs):
    new_ref, kept_v = refs[pieces:]
    gather_pieces(me_ref, refs[:pieces], kept_v)
    kept = halves(kept_v[...])
    pair = (top_ref[...], rest_ref[...])
    for cut in cuts_of(kept_v.shape[1], 384):
        rebuilt = dot3((kept[0][:, cut], kept[1][:, cut]), pair, CONTRACT_ROWS)
        new_ref[cut] = 0.95 * mom_ref[layer, cut] + rebuilt


def pick_kernel(me_ref, a0, b0, a1, b1, out_ref):
    odd = (me_ref[0] & 1) == 1
    out_ref[...] = jnp.where(odd, a1[...] + b1[...], a0[...] + b0[...])


def chain_kernel(me_ref, gram_one, gram_two, one_ref, two_ref, top_ref, rest_ref, out_ref):
    layer = me_ref[0] & 1
    pair = (top_ref[layer], rest_ref[layer])
    side = dot3(halves(one_ref[...] + two_ref[...]), pair, CONTRACT_ROWS)
    gram = 0.9025 * (gram_one[...] + gram_two[...]) + (side + side.T)
    row = lax.broadcasted_iota(jnp.int32, gram.shape, 0)
    column = lax.broadcasted_iota(jnp.int32, gram.shape, 1)
    eye = (row == column).astype(f32)
    norm = jnp.sqrt(jnp.sum(gram * eye, keepdims=True)) + 1e-07
    inverse = 1.0 / norm
    gram = gram * (inverse * inverse)
    chain = None
    for step in range(NS_STEPS):
        gram_pair = halves(gram)
        poly = ns_b * gram + ns_c * dot3(gram_pair, gram_pair)
        poly_pair = halves(poly)
        if chain is None:
            chain = poly + ns_a * eye
        else:
            chain = ns_a * chain + dot3(halves(chain), poly_pair)
        if step + 1 < NS_STEPS:
            turn = ns_a * gram + dot3(gram_pair, poly_pair)
            gram = ns_a * turn + dot3(halves(turn), poly_pair)
    out_ref[...] = chain * (0.3 * inverse)


def update_kernel(apart, carried, me_ref, chain_ref, first_ref, second_ref, weight_ref, *refs):
    new_w, new_m, copy_any, fresh_v, low_v, os = refs[carried:]
    layer = (me_ref[0] & 1) ^ apart
    steps = os.shape[1]
    size = fresh_v.shape[0] // steps
    cuts = [pl.ds(i * size, size) for i in range(steps)]
    pair = halves(chain_ref[...])

    def send(source, target, sem, start=True):
        copy = pltpu.make_async_copy(source, target, sem)
        copy.start() if start else copy.wait()

    def moments(start):
        for k, ref in enumerate((first_ref, second_ref)):

            @pl.when(layer == k)
            def _():
                for i, cut in enumerate(cuts):
                    send(ref.at[cut], new_m.at[k, cut], os.at[0, i], start)

    moments(True)
    for i, cut in enumerate(cuts):
        moment = jnp.where(layer == 0, first_ref[cut], second_ref[cut])
        fresh = weight_ref[layer, cut] * (1.0 - 0.1 * 0.01) - dot3(halves(moment), pair)
        fresh_v[cut] = fresh
        low_v[cut] = fresh.astype(bf16)
        send(fresh_v.at[cut], new_w.at[layer, cut], os.at[1, i])
        send(low_v.at[cut], copy_any.at[layer, cut], os.at[2, i])
    moments(False)
    for i, cut in enumerate(cuts):
        send(fresh_v.at[cut], new_w.at[layer, cut], os.at[1, i], False)
        send(low_v.at[cut], copy_any.at[layer, cut], os.at[2, i], False)


def cosine_rows(index, width):
    cols = jnp.arange(width, dtype=f32)
    freq = index.astype(f32)[..., None]
    return jnp.sqrt(2.0 / width) * jnp.cos(jnp.pi * freq * (2.0 * cols + 1.0) / (2.0 * width))


def swap(value, narrow, wide=0):
    rows, columns = lax.axis_size("wide"), lax.axis_size("narrow")
    pairs = [
        (i * columns + j, (i ^ wide) * columns + (j ^ narrow))
        for i in range(rows)
        for j in range(columns)
    ]
    return lax.ppermute(value, ("wide", "narrow"), pairs)


def stages():
    bits = [(0, 1 << k) for k in range((lax.axis_size("wide") - 1).bit_length())]
    rest = [(2, 0)] + bits
    return [[(1, 0)]] + [rest[i : i + 2] for i in range(0, len(rest), 2)]


def partners(value, bits):
    found = [value]
    offsets = [(0, 0)]
    for narrow, wide in bits:
        offsets = offsets + [(n ^ narrow, w ^ wide) for n, w in offsets]
    for narrow, wide in offsets[1:]:
        found.append(swap(value, narrow, wide))
    return found


def tree(values):
    while len(values) > 1:
        values = [values[i] + values[i + 1] for i in range(0, len(values), 2)]
    return values[0]


def add_kernel(*refs):
    refs[-1][...] = tree([ref[...] for ref in refs[:-1]])


def add_up(parts):
    return call(
        add_kernel,
        "add",
        jax.ShapeDtypeStruct(parts[0].shape, parts[0].dtype),
        [VMEM] * len(parts),
        VMEM,
        [],
        parts[0].size,
        4 * parts[0].size,
        limit=2,
    )(*parts)


def sum_all(value, works=()):
    works = list(works)
    for bits in stages():
        value = add_up(partners(value, bits))
        if works:
            value, _ = lax.optimization_barrier((value, works.pop(0)()))
    return value


def moments_kernel(count, *refs):
    parts, out = [ref[...] for ref in refs[:-1]], refs[-1]
    mean = tree([part[0:1] for part in parts]) * (1.0 / len(parts))
    square = tree([part[1:2] for part in parts])
    apart = tree([jnp.square(part[0:1] - mean) for part in parts])
    out[0:1] = mean
    out[1:2] = square + count * apart
    out[2:3] = tree([part[2:3] for part in parts])
    out[3:8] = jnp.zeros((5, mean.shape[1]), f32)


def merge_moments(stats, count, works=()):
    works = list(works)
    for bits in stages():
        if works:
            stats = works.pop(0)(stats)
        parts = partners(stats, bits)
        stats = call(
            functools.partial(moments_kernel, count),
            "moments",
            jax.ShapeDtypeStruct(stats.shape, f32),
            [VMEM] * len(parts),
            VMEM,
            [],
            stats.size,
            4 * stats.size,
            limit=2,
        )(*parts)
        count = len(parts) * count
    return stats


def mom_gram_kernel(me_ref, mom_any, keep_ref, send_ref, mom_v, sems):
    odd = me_ref[0] & 1
    copies = []
    for k, layer in enumerate((1 - odd, odd)):
        copies.append(pltpu.make_async_copy(mom_any.at[layer], mom_v.at[k], sems.at[k]))
        copies[-1].start()
    for k, out in enumerate((send_ref, keep_ref)):
        copies[k].wait()
        pair = halves(mom_v[k])
        out[...] = dot3(pair, pair, CONTRACT_ROWS)


def adam_rows(param, grad, first, second, rate, decay):
    first = 0.9 * first + 0.1 * grad
    second = 0.999 * second + 0.001 * grad * grad
    mhat = first / (1.0 - 0.9**STEP)
    vhat = second / (1.0 - 0.999**STEP)
    return param - rate * (mhat / (jnp.sqrt(vhat) + 1e-08) + decay * param), first, second


def adam_kernel(
    s1, s2, vec, vec_m, vec_v, head, head_m, head_v, bias, bias_m, bias_v, *outs
):
    o_vec, o_vec_m, bottom, top, o_head, o_head_m, o_head_v, o_bias, o_bias_m, o_bias_v = outs
    rows = ((s1, 1, bottom), (s1, 0, bottom), (s2, 1, top), (s2, 0, top))
    for i, (sums, at, second) in enumerate(rows):
        new, first, square = adam_rows(
            vec[i : i + 1], sums[at : at + 1], vec_m[i : i + 1], vec_v[i : i + 1], 0.3, 0.0
        )
        o_vec[i : i + 1] = new
        o_vec_m[i : i + 1] = first
        second[i & 1 : (i & 1) + 1] = square
    classes = head.shape[0]
    o_head[...], o_head_m[...], o_head_v[...] = adam_rows(
        head[...], s1[8 : 8 + classes], head_m[...], head_v[...], 0.03, 0.01
    )
    o_bias[...], o_bias_m[...], o_bias_v[...] = adam_rows(
        bias[...], s1[24:25, 0:classes], bias_m[...], bias_v[...], 0.3, 0.0
    )


def call(kernel, name, outs, in_specs, out_specs, scratch, flops, moved, limit=10, **more):
    return pl.pallas_call(
        kernel,
        name=name,
        out_shape=outs,
        in_specs=in_specs,
        out_specs=out_specs,
        scratch_shapes=scratch,
        cost_estimate=pl.CostEstimate(flops=flops, bytes_accessed=moved, transcendentals=0),
        compiler_params=pltpu.CompilerParams(vmem_limit_bytes=limit * MIB),
        **more,
    )


def held(*values):
    return [pltpu.with_memory_space_constraint(value, pltpu.VMEM) for value in values]


def dma(n):
    return pltpu.SemaphoreType.DMA((n,))


def per_device(
    images,
    labels,
    class_weight,
    basis_index,
    atom_mask,
    conv_weight,
    conv_momentum,
    batch_norm_params,
    norm_first,
    norm_second,
    head_weight,
    head_first,
    head_second,
    head_bias,
    bias_first,
    bias_second,
):
    count, width = images.shape[0], images.shape[3]
    local_rows = conv_weight.shape[1]
    rank = basis_index.shape[1]
    classes = head_weight.shape[0]
    wides = lax.axis_size("wide")
    pixel_count = count * PIX * wides * lax.axis_size("narrow")
    me_narrow = lax.axis_index("narrow")
    low_wides = min(8, wides)
    me = jnp.stack([me_narrow, lax.axis_index("wide") & (low_wides - 1)]).astype(jnp.int32)
    sds = jax.ShapeDtypeStruct
    field16 = pltpu.VMEM((PIX, count, width), bf16)
    field32 = (pltpu.VMEM((SIDE, count, width), f32),) * SIDE
    small = sds((8, width), f32)
    weight_v = pltpu.VMEM((TAPS * width, width), bf16)
    conv_flops = 2 * 100 * count * width * width
    field_bytes = 4 * PIX * count * width

    low_weight = conv_weight.astype(bf16)

    def tie(*values):
        return lax.optimization_barrier(values)

    own = low_weight[0]
    near, far = swap(own, 1), swap(own, 2)
    x = images.reshape(count, PIX, width).transpose(1, 0, 2)
    onehot = labels[:, None] == jnp.arange(classes, dtype=jnp.int32)[None, :]
    weight_sum = jnp.sum(jnp.where(onehot, class_weight.astype(f32)[None, :], 0.0))
    extra = jnp.full((1, width), weight_sum, f32)
    bases = cosine_rows(basis_index, width)
    basis_top = bases.astype(bf16)
    basis_rest = (bases - basis_top.astype(f32)).astype(bf16)
    masks = atom_mask[:, 0].transpose(0, 2, 1).astype(bf16)
    head_low = jnp.pad(head_weight.astype(bf16), ((0, 128 - classes), (0, 0)))
    head_bias_row = jnp.pad(head_bias, (0, 128 - classes))[None]
    class_row = jnp.pad(class_weight.astype(f32), (0, 128 - classes))[None]
    prepared = (
        [low_weight[1], masks[0], masks[1]]
        + [basis_top[0], basis_top[1], basis_rest[0], basis_rest[1], basis_top, basis_rest]
        + [head_low, head_bias_row, class_row, labels[None]]
        + [row[None] for row in (head_bias, bias_first, bias_second)]
    )
    gram_keep, gram_send = call(
        mom_gram_kernel,
        "mom_gram",
        (sds((width, width), f32),) * 2,
        [SMEM, ANY],
        (VMEM, VMEM),
        [pltpu.VMEM((2, local_rows, width), f32), dma(2)],
        12 * local_rows * width * width,
        8 * local_rows * width,
        limit=8,
    )(me, conv_momentum)
    x, extra, me, far, prepared, gram_keep, gram_send = tie(
        x, extra, me, far, prepared, gram_keep, gram_send
    )
    first_weight = (own, near, far, swap(far, 1))
    gram_mine = add_up([gram_keep, swap(gram_send, 1)])
    second_own, mask0, mask1, top0, top1, rest0, rest1, bases_top, bases_rest = prepared[:9]
    head_low, head_bias_row, class_row, label_row, bias_row, bias_m_row, bias_v_row = prepared[9:]
    basis_top, basis_rest = (top0, top1), (rest0, rest1)
    second_near, second_far = swap(second_own, 1), swap(second_own, 2)

    *hid1, stats1 = call(
        conv_first_kernel,
        "conv_first",
        (*field32, small),
        [SMEM, VMEM, VMEM, ANY, ANY, ANY, ANY],
        (VMEM,) * 5,
        [weight_v, dma(4)],
        conv_flops,
        2 * field_bytes,
        limit=7,
        )(me, extra, x, *first_weight)
    hid1 = held(*hid1)
    late = {}

    def last_weight(stats):
        stats, late["far"] = tie(stats, second_far)
        late["last"] = swap(late["far"], 1)
        return stats

    stats1 = merge_moments(stats1, count * PIX, (lambda s: s, lambda s: s, last_weight))

    stats1, gram_mine = tie(stats1, gram_mine)
    gram_other = swap(gram_mine, 2)
    second_weight = (second_own, second_near, late["far"], late["last"])

    outs = call(
        functools.partial(conv_second_kernel, pixel_count),
        "conv_second",
        (*field32, field16, *(pltpu.VMEM((3, width, width), bf16),) * 3, small),
        [SMEM] + [VMEM] * 6 + [ANY] * 4,
        (VMEM,) * 9,
        [weight_v, dma(4)],
        conv_flops,
        3 * field_bytes,
        limit=7,
        )(me, stats1, batch_norm_params, *hid1, *second_weight)
    hid2, z1, turned_weight = held(*outs[:4]), held(outs[4])[0], held(*outs[5:8])
    stats2 = outs[8]
    stats2 = merge_moments(stats2, count * PIX)
    stats2, gram_other = tie(stats2, gram_other)

    *slope2, dp, sums2, aux = call(
        functools.partial(head_kernel, pixel_count, classes),
        "head",
        (*field32, sds((count, width), f32), small, sds((24, width), f32)),
        [VMEM] * 11,
        (VMEM,) * 7,
        [
            pltpu.VMEM((count, width), bf16),
            pltpu.VMEM((count, width), f32),
            pltpu.VMEM((count, width), f32),
        ],
        conv_flops // 3,
        3 * field_bytes,
        limit=4,
        )(
        stats2,
        batch_norm_params,
        head_low,
        head_bias_row,
        label_row,
        class_row,
        x,
        *hid2,
    )
    slope2 = held(*slope2)
    sums2 = sum_all(sums2)
    sums2, mask0, mask1 = tie(sums2, mask0, mask1)
    gram_pair = (gram_mine, gram_other)
    mask_parts = [(mask, swap(mask, 1), swap(mask, 2)) for mask in (mask1, mask0)]

    dh2, *dy1, sums1 = call(
        functools.partial(second_grad_kernel, pixel_count),
        "second_grad",
        (field16, *field32, sds((32, width), f32)),
        [VMEM] * 21,
        (VMEM,) * 6,
        [],
        conv_flops,
        5 * field_bytes,
        input_output_aliases={10 + p: 1 + p for p in range(SIDE)},
        limit=3,
        )(stats1, stats2, sums2, batch_norm_params, dp, aux, *hid2, *slope2, *hid1, *turned_weight)

    dh2, dy1 = held(dh2)[0], held(*dy1)
    sums1, far1, far0 = tie(sums1, mask_parts[0][2], mask_parts[1][2])
    masks = [
        (own, near, far, swap(far, 1))
        for (own, near, _), far in zip(mask_parts[::-1], (far0, far1))
    ]
    rows = rank // low_wides
    depth = low_wides // 2
    def coef_outs(outer):
        inner = 4 * depth // outer
        return (sds((inner, rows, local_rows), f32),) * outer + (
            sds((outer, inner, rows, local_rows), f32),
        )

    turned_v = pltpu.VMEM((PIX, 2 * rank, count), bf16)
    basis_v = pltpu.VMEM((width, 2 * rank), bf16)
    sum_v = pltpu.VMEM((TAPS, rank, width), f32)
    mask_v = pltpu.VMEM((4, rank, local_rows), bf16)
    coef_v = pltpu.VMEM((4, rank, local_rows), f32)
    results = {}

    def second_top():
        results["top"] = call(
            coef_top_kernel,
            "coef_top",
            sds((TAPS, rank, width), f32),
            [VMEM] * 4,
            VMEM,
            [basis_v, turned_v],
            conv_flops // 4,
            field_bytes,
        limit=3,
        )(basis_top[1], basis_rest[1], dh2, z1)
        return results["top"]

    def second_bottom():
        results["second"] = call(
            coef_bottom_kernel,
            "coef_bottom",
            coef_outs(2),
            [SMEM] + [VMEM] * 5 + [ANY] * 4,
            (VMEM,) * 3,
            [basis_v, turned_v, sum_v, mask_v, coef_v, dma(4)],
            conv_flops // 4,
            field_bytes,
            limit=9,
        )(me, basis_top[1], basis_rest[1], results["top"], dh2, z1, *masks[1])
        return results["second"]

    def core_stage(outs):
        *keeps, send = outs
        return call(
            add_parts_kernel,
            "add_parts",
            [sds(keep.shape, f32) for keep in keeps],
            [VMEM] * (len(keeps) + 1),
            [VMEM] * len(keeps),
            [],
            rank * local_rows * 2,
            rank * local_rows * 24,
        )(*keeps, swap(send, 1))

    def reduce_stage(parts, offsets, cuts, after=()):
        received = [swap(part, *bits) for part, bits in zip(parts[1:], offsets[1:])]
        received, _ = tie(received, after)
        size = parts[0].shape[0] // cuts
        return call(
            functools.partial(add_pieces_kernel, len(parts)),
            "add_pieces",
            [sds((size, rows, local_rows), f32)] * cuts,
            [VMEM] * len(parts),
            [VMEM] * cuts,
            [],
            rank * local_rows,
            rank * local_rows * 12,
        )(parts[0], *received)

    def high_bits(own):
        own = own.reshape(rows, local_rows)
        bit = low_wides
        while bit < wides:
            own = add_up([own, swap(own, 0, bit)])
            bit = 2 * bit
        return own

    def spread(own):
        found = {0: own}
        for z in range(1, depth):
            found[2 * z] = swap(own, 0, 2 * z)
        found[1] = swap(own, 0, 1)
        for z in range(1, depth):
            found[2 * z + 1] = swap(found[2 * z], 0, 1)
        return [found[k] for k in range(low_wides)]

    def gram_stage(pieces, layer):
        parts = call(
            functools.partial(gram_parts_kernel, layer, low_wides),
            "gram_parts",
            sds((rank, width), f32),
            [SMEM] + [VMEM] * (3 + low_wides),
            VMEM,
            [pltpu.VMEM((rank, local_rows), f32)],
            6 * rank * local_rows * (width + rank),
            4 * local_rows * width,
        )(me, basis_top[layer], basis_rest[layer], conv_momentum, *pieces)
        return parts, swap(parts, 1)

    whole = sds((2, local_rows, width), f32)
    block_v = pltpu.VMEM((local_rows, width), f32)

    def moment_stage(pieces, layer):
        return call(
            functools.partial(moment_kernel, layer, low_wides),
            "moment",
            sds((local_rows, width), f32),
            [SMEM] + [VMEM] * (3 + low_wides),
            VMEM,
            [pltpu.VMEM((rank, local_rows), f32)],
            6 * local_rows * width * rank,
            8 * local_rows * width,
        )(me, basis_top[layer], basis_rest[layer], conv_momentum, *pieces)

    def update_stage(apart, chain, previous):
        carried = len(previous)
        return call(
            functools.partial(update_kernel, apart, carried),
            "update",
            (whole, whole, sds((2, local_rows, width), bf16)),
            [SMEM] + [VMEM] * 4 + [ANY] * carried,
            (ANY,) * 3,
            [block_v, pltpu.VMEM((local_rows, width), bf16), pltpu.SemaphoreType.DMA((3, 3))],
            6 * local_rows * width * width,
            16 * local_rows * width,
            limit=16,
            input_output_aliases={5 + i: i for i in range(carried)},
        )(me, chain, moment1, moment2, conv_weight, *previous)

    def second_core():
        results["parts"] = core_stage(results["second"])
        return results["parts"]

    def second_both():
        second_top()
        return second_bottom()

    sums1 = sum_all(sums1, (second_both, second_core))
    first = call(
        functools.partial(coef_first_kernel, pixel_count),
        "coef_first",
        coef_outs(4),
        [SMEM] + [VMEM] * 14 + [ANY] * 4,
        (VMEM,) * 5,
        [basis_v, turned_v, sum_v, mask_v, coef_v, dma(4)],
        conv_flops // 2,
        3 * field_bytes,
        limit=9,
    )(me, basis_top[0], basis_rest[0], stats1, sums1, batch_norm_params, x, *dy1, *hid1, *masks[0])

    parts1 = core_stage(first)
    parts2 = results["parts"]
    pieces1 = reduce_stage(parts1, PLANE, 4)
    pieces2 = reduce_stage(parts2, NEAR, 4, pieces1)
    (own1,) = reduce_stage(pieces1, DEPTH, 1)
    halves2 = reduce_stage(pieces2, PLANE, 2)
    own1 = high_bits(own1)
    all1 = spread(own1)
    (own2,) = reduce_stage(halves2, FAR, 1, own1)
    own2 = high_bits(own2)
    all2 = spread(own2)
    grams2 = gram_stage(all2, 1)
    row, pair, column = sds((4, width), f32), sds((2, width), f32), sds((classes, width), f32)
    line = sds((1, classes), f32)
    small_outs = call(
        adam_kernel,
        "adam",
        (row, row, pair, pair, column, column, column, line, line, line),
        [VMEM] * 11,
        (VMEM,) * 10,
        [],
        100 * classes * width,
        40 * classes * width,
        limit=2,
    )(
        sums1,
        sums2,
        batch_norm_params,
        norm_first,
        norm_second,
        head_weight,
        head_first,
        head_second,
        bias_row,
        bias_m_row,
        bias_v_row,
    )
    small_outs = (*small_outs, sums1[25, 0], stats1[2, 0])
    moment2 = moment_stage(all2, 1)
    grams1 = gram_stage(all1, 0)
    mine = call(
        pick_kernel,
        "pick",
        sds((rank, width), f32),
        [SMEM] + [VMEM] * 4,
        VMEM,
        [],
        rank * width,
        20 * rank * width,
        limit=4,
    )(me, *grams1, *grams2)
    other = swap(mine, 2)
    moment1 = moment_stage(all1, 0)
    other, moment1, moment2, small_outs = tie(other, moment1, moment2, small_outs)
    chain = call(
        chain_kernel,
        "chain",
        sds((width, width), f32),
        [SMEM] + [VMEM] * 6,
        VMEM,
        [],
        6 * 17 * width**3,
        8 * width * width,
        limit=24,
    )(me, *gram_pair, mine, other, bases_top, bases_rest)
    far_chain = swap(chain, 1)
    outs = update_stage(0, chain, ())
    new_weight, moment, low_copy = update_stage(1, far_chain, outs)

    vec, vec_m, bottom, top, head_new, head_m, head_v, bias_new, bias_m, bias_v = small_outs[:10]
    return (
        small_outs[10],
        small_outs[11],
        new_weight,
        moment,
        low_copy,
        vec,
        vec_m,
        bottom,
        top,
        head_new,
        head_m,
        head_v,
        bias_new[0],
        bias_m[0],
        bias_v[0],
    )


def solution(mesh):
    rep = P()
    rows = P(None, "narrow", None)
    return jax.shard_map(
        per_device,
        mesh=mesh,
        in_specs=(
            P(("wide", "narrow"), None, None, None),
            P(("wide", "narrow")),
            rep,
            rep,
            P(None, "wide", "narrow", None),
            rows,
            rows,
        )
        + (rep,) * 9,
        out_specs=(rep, rep, rows, rows, rows) + (rep,) * 10,
        check_vma=False,
    )
```

```python
import functools

import jax
import jax.numpy as jnp
from jax import lax
from jax.experimental import pallas as pl
from jax.experimental.pallas import tpu as pltpu
from jax.sharding import PartitionSpec as P

SIDE = 4
PIX = SIDE * SIDE
TAPS = 9
NS_STEPS = 5
STEP = 5

f32 = jnp.float32
bf16 = jnp.bfloat16
highest = lax.Precision.HIGHEST
norm_eps = 1e-05
smooth = 0.1
ns_a, ns_b, ns_c = (3.4445, -4.775, 2.0315)
MIB = 1 << 20

ANY = pl.BlockSpec(memory_space=pl.ANY)
VMEM = pl.BlockSpec(memory_space=pltpu.VMEM)
SMEM = pl.BlockSpec(memory_space=pltpu.SMEM)


class Field:
    def __init__(self, refs):
        self.refs = refs

    def __getitem__(self, pixel):
        return self.refs[pixel // SIDE].at[pixel % SIDE]


def out_taps(pixel):
    p, q = divmod(pixel, SIDE)
    found = []
    for tap in range(TAPS):
        a, b = divmod(tap, 3)
        pp, qq = p + a - 1, q + b - 1
        if 0 <= pp < SIDE and 0 <= qq < SIDE:
            found.append((tap, pp * SIDE + qq))
    return found


def in_taps(pixel):
    found = []
    for out in range(PIX):
        for tap, source in out_taps(out):
            if source == pixel:
                found.append((tap, out))
    return found


def sigma_of(value):
    return 0.5 * jnp.tanh(0.5 * value) + 0.5


def weight_loads(me_ref, pieces, target, sems):
    me = me_ref[0]
    copies = []
    rows = pieces[0].shape[0]
    for k, piece in enumerate(pieces):
        start = pl.multiple_of((me ^ k) * rows, rows)
        copies.append(pltpu.make_async_copy(piece, target.at[pl.ds(start, rows)], sems.at[k]))
        copies[-1].start()
    return copies


def row_of(p):
    return list(range(p * SIDE, (p + 1) * SIDE)) if 0 <= p < SIDE else []


def cuts_of(count, size=32):
    return [slice(i, i + size) for i in range(0, count, size)]


def fold(value):
    return jnp.sum(value.reshape(-1, 8, value.shape[1]), axis=0)


def block_moments(block):
    cuts = cuts_of(block.shape[0])
    total = sum(fold(block[cut]) for cut in cuts)
    mean = jnp.sum(total, axis=0, keepdims=True) * (1.0 / block.shape[0])
    square = sum(fold(jnp.square(block[cut] - mean)) for cut in cuts)
    return mean, jnp.sum(square, axis=0, keepdims=True)


def store_moments(stats_ref, parts, rows, extra):
    mean = sum(m for m, _ in parts) * (1.0 / len(parts))
    square = sum(s for _, s in parts) + rows * sum(jnp.square(m - mean) for m, _ in parts)
    stats_ref[0:1] = mean
    stats_ref[1:2] = square
    stats_ref[2:3] = extra
    stats_ref[3:8] = jnp.zeros((5, mean.shape[1]), f32)


def conv_pixel(source, weight, pixel, width):
    total = None
    for tap, read in out_taps(pixel):
        part = jnp.dot(
            source[read][...], weight[tap * width : (tap + 1) * width], preferred_element_type=f32
        )
        total = part if total is None else total + part
    return total


def conv_first_kernel(me_ref, extra_ref, x_ref, w0, w1, w2, w3, h0, h1, h2, h3, stats_ref, w_v, ws):
    width = x_ref.shape[2]
    x_field, hid = Field([x_ref.at[pl.ds(p * SIDE, SIDE)] for p in range(SIDE)]), Field((h0, h1, h2, h3))
    for copy in weight_loads(me_ref, (w0, w1, w2, w3), w_v, ws):
        copy.wait()
    parts = []
    for pixel in range(PIX):
        hid[pixel][...] = conv_pixel(x_field, w_v, pixel, width)
        if pixel > 0:
            parts.append(block_moments(hid[pixel - 1]))
    parts.append(block_moments(hid[PIX - 1]))
    store_moments(stats_ref, parts, x_ref.shape[1], extra_ref[...])


def norm_rows(stats_ref, pixel_count):
    mean = stats_ref[0:1]
    return mean, lax.rsqrt(stats_ref[1:2] * (1.0 / pixel_count) + norm_eps)


def half_affine(scale, gain, shift):
    return 0.5 * (gain * scale), 0.5 * shift


def conv_second_kernel(pixel_count, me_ref, stats_in, params, *refs):
    h, weights, hid = Field(refs[:4]), refs[4:8], Field(refs[8:12])
    z_ref = refs[12]
    turned_refs = refs[13:16]
    stats_ref, w_v, ws = refs[16:]
    count, width = z_ref.shape[1:]
    z = Field([z_ref.at[pl.ds(p * SIDE, SIDE)] for p in range(SIDE)])
    wait_w = weight_loads(me_ref, weights, w_v, ws)
    mean, scale = norm_rows(stats_in, pixel_count)
    slope, offset = half_affine(scale, params[0:1], params[1:2])

    def activate(pixel):
        for cut in cuts_of(count):
            half = (h[pixel][cut] - mean) * slope + offset
            z[pixel][cut] = (half + half * jnp.tanh(half)).astype(bf16)

    first = SIDE + 2
    for pixel in range(first):
        activate(pixel)
    for copy in wait_w:
        copy.wait()
    parts = []
    for pixel in range(PIX):
        hid[pixel][...] = conv_pixel(z, w_v, pixel, width)
        if pixel + first < PIX:
            activate(pixel + first)
        if pixel < TAPS:
            turned_refs[pixel // 3][pixel % 3] = w_v[pixel * width : (pixel + 1) * width].T
        if pixel > 0:
            parts.append(block_moments(hid[pixel - 1]))
    parts.append(block_moments(hid[PIX - 1]))
    share = PIX * count / pixel_count
    store_moments(stats_ref, parts, count, stats_in[2:3] * share)


def head_kernel(
    pixel_count,
    classes,
    stats_in,
    params,
    head_ref,
    bias_ref,
    label_ref,
    class_ref,
    x_ref,
    *refs,
):
    h, slopes = Field(refs[:4]), Field(refs[4:8])
    dp_ref, sums_ref, aux_ref, pool_v, s1_v, s2_v = refs[8:]
    count, width = x_ref.shape[1:]
    rows = 32
    mean, scale = norm_rows(stats_in, pixel_count)
    slope_row, offset_row = half_affine(scale, params[2:3], params[3:4])

    def body(i, carry):
        here = pl.ds(pl.multiple_of(i * rows, rows), rows)
        for lane in range(0, width, 128):
            cut = slice(lane, lane + 128)
            slope, offset, middle = slope_row[:, cut], offset_row[:, cut], mean[:, cut]
            pool = jnp.zeros((rows, 128), f32)
            s1 = jnp.zeros((rows, 128), f32)
            s2 = jnp.zeros((rows, 128), f32)
            for pixel in range(PIX):
                hid = h[pixel][here, cut] - middle
                half = (hid * slope + offset) + 0.5 * x_ref[pixel, here, cut].astype(f32)
                turn = jnp.tanh(half)
                act = half + half * turn
                double = (1.0 + turn) + act * (1.0 - turn)
                slopes[pixel][here, cut] = double
                pool = pool + act
                s1 = s1 + double
                s2 = s2 + double * hid
            pool_v[here, cut] = (pool * (1.0 / PIX)).astype(bf16)
            s1_v[here, cut] = s1
            s2_v[here, cut] = s2
        return carry

    lax.fori_loop(0, count // rows, body, 0)
    pooled = pool_v[...]
    head = head_ref[...]
    logits = (
        lax.dot_general(pooled, head, (((1,), (1,)), ((), ())), preferred_element_type=f32)
        + bias_ref[...]
    )
    lane_index = lax.broadcasted_iota(jnp.int32, logits.shape, 1)
    valid = lane_index < classes
    label = jnp.broadcast_to(label_ref[...].astype(f32), logits.shape[::-1]).T
    onehot = (lane_index.astype(f32) == label).astype(f32)
    weight_each = jnp.sum(onehot * class_ref[...], axis=1, keepdims=True)
    top = jnp.max(jnp.where(valid, logits, -jnp.inf), axis=1, keepdims=True)
    moved = jnp.where(valid, logits - top, 0.0)
    powers = jnp.where(valid, jnp.exp(moved), 0.0)
    total = jnp.sum(powers, axis=1, keepdims=True)
    logp = jnp.where(valid, moved - jnp.log(total), 0.0)
    target = jnp.where(valid, (1.0 - smooth) * onehot + smooth / classes, 0.0)
    per_image = -jnp.sum(target * logp, axis=1, keepdims=True)
    loss = jnp.sum(weight_each * per_image, axis=0, keepdims=True)
    weight_total = stats_in[2:3, 0:1]
    dlogits = weight_each * (powers / total - target) / weight_total
    dp = (
        jnp.dot(dlogits, head.astype(f32), precision=highest, preferred_element_type=f32)
        * (0.5 / PIX)
    )
    dp_ref[...] = dp
    shift_sum = jnp.sum(dp * s1_v[...], axis=0, keepdims=True)
    raw_sum = jnp.sum(dp * s2_v[...], axis=0, keepdims=True)
    sums_ref[0:1] = shift_sum
    sums_ref[1:2] = raw_sum * scale
    sums_ref[2:8] = jnp.zeros((6, width), f32)
    head_grad = lax.dot_general(
        dlogits,
        pooled.astype(f32),
        (((0,), (0,)), ((), ())),
        precision=highest,
        preferred_element_type=f32,
    )
    aux_ref[...] = jnp.zeros(aux_ref.shape, f32)
    aux_ref[2 : 2 + classes] = head_grad[:classes]
    aux_ref[2 + classes : 3 + classes, 0:128] = jnp.sum(dlogits, axis=0, keepdims=True)
    aux_ref[3 + classes : 4 + classes, 0:128] = jnp.broadcast_to(loss, (1, 128))


def second_grad_kernel(
    pixel_count,
    stats1,
    stats2,
    sums2,
    params,
    dp_ref,
    aux_ref,
    *refs,
):
    h2, slopes, h1, weights = Field(refs[:4]), Field(refs[4:8]), Field(refs[8:12]), refs[12:15]
    dh_ref, dy, sums_ref = refs[15], Field(refs[16:20]), refs[20]
    count, width = dh_ref.shape[1:]
    mean2, scale2 = norm_rows(stats2, pixel_count)
    outer = params[2:3] * scale2
    gain_part = -sums2[1:2] * (1.0 / pixel_count) * scale2 * outer
    shift_part = -sums2[0:1] * (1.0 / pixel_count) * outer
    mean1, scale1 = norm_rows(stats1, pixel_count)
    slope1, offset1 = half_affine(scale1, params[0:1], params[1:2])

    def hidden_grad(pixel):
        for cut in cuts_of(count):
            spread = (dp_ref[cut] * outer) * slopes[pixel][cut]
            dh_ref[pixel, cut] = (spread + ((h2[pixel][cut] - mean2) * gain_part + shift_part)).astype(bf16)

    def gather_grads(pixel):
        total = None
        for tap, out in in_taps(pixel):
            weight = weights[tap // 3][tap % 3]
            part = jnp.dot(dh_ref[out], weight, preferred_element_type=f32)
            total = part if total is None else total + part
        dy[pixel][...] = total

    def finish(pixel, shift_sum, raw_sum):
        for cut in cuts_of(count):
            hid = h1[pixel][cut] - mean1
            half = hid * slope1 + offset1
            turn = jnp.tanh(half)
            act = half + half * turn
            grad = dy[pixel][cut] * ((1.0 + turn) + act * (1.0 - turn))
            dy[pixel][cut] = grad
            shift_sum = shift_sum + fold(grad)
            raw_sum = raw_sum + fold(grad * hid)
        return shift_sum, raw_sum

    shift_sum = jnp.zeros((8, width), f32)
    raw_sum = jnp.zeros((8, width), f32)
    first = SIDE + 2
    for pixel in range(first):
        hidden_grad(pixel)
    for pixel in range(PIX):
        gather_grads(pixel)
        if pixel + first < PIX:
            hidden_grad(pixel + first)
        if pixel > 0:
            shift_sum, raw_sum = finish(pixel - 1, shift_sum, raw_sum)
    shift_sum, raw_sum = finish(PIX - 1, shift_sum, raw_sum)
    shift_sum = 0.5 * jnp.sum(shift_sum, axis=0, keepdims=True)
    raw_sum = 0.5 * jnp.sum(raw_sum, axis=0, keepdims=True)
    sums_ref[...] = aux_ref[...]
    sums_ref[0:1] = shift_sum
    sums_ref[1:2] = raw_sum * scale1


def coef_rows(spans, grad_of, source_ref, top_ref, rest_ref, basis_v, turned, add):
    rank = top_ref.shape[0]
    basis_v[:, :rank] = top_ref[...].T
    basis_v[:, rank:] = rest_ref[...].T

    def project(pixel):
        both = jnp.dot(grad_of(pixel), basis_v[...], preferred_element_type=f32)
        low = both[:, :rank] + both[:, rank:]
        top = low.astype(bf16)
        rest = (low - top.astype(f32)).astype(bf16)
        turned[pixel, :rank] = top.T
        turned[pixel, rank:] = rest.T

    for pixel in row_of(spans[0]):
        project(pixel)
    for p in spans:
        todo = row_of(p + 1) if p + 1 in spans else []
        for a in (1, 0, 2):
            if not 0 <= p + a - 1 < SIDE:
                continue
            for b in range(3):
                total = None
                for q in range(SIDE):
                    if 0 <= q + b - 1 < SIDE:
                        part = jnp.dot(
                            turned[p * SIDE + q],
                            source_ref[(p + a - 1) * SIDE + q + b - 1],
                            preferred_element_type=f32,
                        )
                        total = part if total is None else total + part
                add(p, 3 * a + b, total[:rank] + total[rank:])
                if todo:
                    project(todo.pop(0))


def store_coef(coef_v, mask_v, tap, coef):
    part_width = coef_v.shape[2]
    width = coef.shape[1]
    at = tap * width
    while at < (tap + 1) * width:
        j = at // part_width
        end = min((j + 1) * part_width, (tap + 1) * width)
        cut = slice(at - j * part_width, end - j * part_width)
        coef_v[j, :, cut] = (
            coef[:, at - tap * width : end - tap * width] * mask_v[j, :, cut].astype(f32)
        )
        at = end


PLANE = [(2 * (k & 1), k >> 1) for k in range(4)]
DEPTH = [(0, 2 * k) for k in range(4)]
NEAR, FAR = [(0, 0), (0, 2)], [(0, 0), (0, 4)]


def send_coef(me_ref, coef_v, keeps, send_ref, outer, inner):
    me, wide = me_ref[0], me_ref[1]
    rows = keeps[0].shape[1]
    for core in (1, 0):
        for i, (n0, w0) in enumerate(outer):
            for j, (n1, w1) in enumerate(inner):
                start = pl.multiple_of((wide ^ (w0 ^ w1)) * rows, rows)
                piece = coef_v[me ^ (core ^ n0 ^ n1), pl.ds(start, rows)]
                if core:
                    send_ref[i, j] = piece
                else:
                    keeps[i][j] = piece


def mask_loads(me_ref, pieces, target, sems):
    copies = [
        pltpu.make_async_copy(piece, target.at[me_ref[0] ^ k], sems.at[k])
        for k, piece in enumerate(pieces)
    ]
    for copy in copies:
        copy.start()
    return copies


def coef_top_kernel(top_ref, rest_ref, dh_ref, z_ref, sum_ref, basis_v, turned):
    seen = set()

    def add(p, tap, part):
        sum_ref[tap] = sum_ref[tap] + part if tap in seen else part
        seen.add(tap)

    coef_rows((0, 1), lambda i: dh_ref[i], z_ref, top_ref, rest_ref, basis_v, turned, add)


def coef_bottom_kernel(
    me_ref, top_ref, rest_ref, sum_ref, dh_ref, z_ref, *refs
):
    masks, keeps, refs = refs[:4], refs[4:6], refs[6:]
    send_ref, basis_v, turned, sum_v, mask_v, coef_v, ms = refs
    wait_mask = mask_loads(me_ref, masks, mask_v, ms)
    seen = set()

    def add(p, tap, part):
        if p == 3 and tap == 3:
            for copy in wait_mask:
                copy.wait()
        total = (sum_v if tap in seen else sum_ref)[tap] + part
        seen.add(tap)
        if p == 3:
            store_coef(coef_v, mask_v, tap, total)
        else:
            sum_v[tap] = total

    coef_rows((2, 3), lambda i: dh_ref[i], z_ref, top_ref, rest_ref, basis_v, turned, add)
    for tap in (6, 7, 8):
        store_coef(coef_v, mask_v, tap, sum_v[tap])
    inner = [(n, w ^ far) for n, w in PLANE for _, far in FAR]
    send_coef(me_ref, coef_v, keeps, send_ref, NEAR, inner)


def coef_first_kernel(
    pixel_count,
    me_ref,
    top_ref,
    rest_ref,
    stats1,
    sums1,
    params,
    x_ref,
    *refs,
):
    dy, h1, masks, keeps = Field(refs[:4]), Field(refs[4:8]), refs[8:12], refs[12:16]
    send_ref, basis_v, turned, sum_v, mask_v, coef_v, ms = refs[16:]
    wait_mask = mask_loads(me_ref, masks, mask_v, ms)
    mean, scale = norm_rows(stats1, pixel_count)
    outer = params[0:1] * scale
    gain_part = -sums1[1:2] * (1.0 / pixel_count) * scale * outer
    shift_part = -sums1[0:1] * (1.0 / pixel_count) * outer
    half_outer = 0.5 * outer
    seen = set()

    def grad_of(pixel):
        return jnp.concatenate(
            [
                (
                    dy[pixel][cut] * half_outer
                    + ((h1[pixel][cut] - mean) * gain_part + shift_part)
                ).astype(bf16)
                for cut in cuts_of(x_ref.shape[1])
            ],
            axis=0,
        )

    def add(p, tap, part):
        if p == 3 and tap == 3:
            for copy in wait_mask:
                copy.wait()
        total = sum_v[tap] + part if tap in seen else part
        seen.add(tap)
        if p == 3:
            store_coef(coef_v, mask_v, tap, total)
        else:
            sum_v[tap] = total

    coef_rows(range(SIDE), grad_of, x_ref, top_ref, rest_ref, basis_v, turned, add)
    for tap in (6, 7, 8):
        store_coef(coef_v, mask_v, tap, sum_v[tap])
    send_coef(me_ref, coef_v, keeps, send_ref, PLANE, DEPTH)


def add_parts_kernel(*refs):
    count = len(refs) // 2
    keeps, other, outs = refs[:count], refs[count], refs[count + 1 :]
    for part, (keep, out) in enumerate(zip(keeps, outs)):
        out[...] = keep[...] + other[part]


def add_pieces_kernel(received, *refs):
    parts, outs = refs[:received], refs[received:]
    size = parts[0].shape[0] // len(outs)
    for k, out in enumerate(outs):
        cut = pl.ds(k * size, size)
        total = tree([part[cut] for part in parts])
        out[...] = total.reshape(out.shape)


def halves(value):
    top = value.astype(bf16)
    return top, (value - top.astype(f32)).astype(bf16)


def dot3(left, right, dims=(((1,), (0,)), ((), ()))):
    (a, b), (c, d) = left, right

    def dot(x, y):
        return lax.dot_general(x, y, dims, preferred_element_type=f32)

    return dot(a, c) + (dot(a, d) + dot(b, c))


CONTRACT_ROWS = (((0,), (0,)), ((), ()))
CONTRACT_COLUMNS = (((1,), (1,)), ((), ()))


def gather_pieces(me_ref, pieces, target):
    rows = pieces[0].shape[0]
    for k, piece in enumerate(pieces):
        start = pl.multiple_of((me_ref[1] ^ k) * rows, rows)
        target[pl.ds(start, rows)] = piece[...]


def gram_parts_kernel(layer, pieces, me_ref, top_ref, rest_ref, mom_ref, *refs):
    out_ref, kept_v = refs[pieces:]
    gather_pieces(me_ref, refs[:pieces], kept_v)
    rank = kept_v.shape[0]
    kept, rest = halves(kept_v[...])
    stacked = jnp.concatenate([kept, rest], axis=0)
    total, extra = None, None
    for cut in cuts_of(kept_v.shape[1], 384):
        top, low = halves(mom_ref[layer, cut])
        one = jnp.dot(stacked[:, cut], top, preferred_element_type=f32)
        two = jnp.dot(kept[:, cut], low, preferred_element_type=f32)
        total = one if total is None else total + one
        extra = two if extra is None else extra + two
    cross = total[:rank] + total[rank:] + extra
    square = dot3((kept, rest), (kept, rest), CONTRACT_COLUMNS)
    out_ref[...] = 0.95 * cross + 0.5 * dot3(halves(square), (top_ref[...], rest_ref[...]))


def moment_kernel(layer, pieces, me_ref, top_ref, rest_ref, mom_ref, *refs):
    new_ref, kept_v = refs[pieces:]
    gather_pieces(me_ref, refs[:pieces], kept_v)
    kept = halves(kept_v[...])
    pair = (top_ref[...], rest_ref[...])
    for cut in cuts_of(kept_v.shape[1], 384):
        rebuilt = dot3((kept[0][:, cut], kept[1][:, cut]), pair, CONTRACT_ROWS)
        new_ref[cut] = 0.95 * mom_ref[layer, cut] + rebuilt


def pick_kernel(me_ref, a0, b0, a1, b1, out_ref):
    odd = (me_ref[0] & 1) == 1
    out_ref[...] = jnp.where(odd, a1[...] + b1[...], a0[...] + b0[...])


def chain_kernel(me_ref, gram_one, gram_two, one_ref, two_ref, top_ref, rest_ref, out_ref):
    layer = me_ref[0] & 1
    pair = (top_ref[layer], rest_ref[layer])
    side = dot3(halves(one_ref[...] + two_ref[...]), pair, CONTRACT_ROWS)
    gram = 0.9025 * (gram_one[...] + gram_two[...]) + (side + side.T)
    row = lax.broadcasted_iota(jnp.int32, gram.shape, 0)
    column = lax.broadcasted_iota(jnp.int32, gram.shape, 1)
    eye = (row == column).astype(f32)
    norm = jnp.sqrt(jnp.sum(gram * eye, keepdims=True)) + 1e-07
    inverse = 1.0 / norm
    gram = gram * (inverse * inverse)
    chain = None
    for step in range(NS_STEPS):
        gram_pair = halves(gram)
        poly = ns_b * gram + ns_c * dot3(gram_pair, gram_pair)
        poly_pair = halves(poly)
        if chain is None:
            chain = poly + ns_a * eye
        else:
            chain = ns_a * chain + dot3(halves(chain), poly_pair)
        if step + 1 < NS_STEPS:
            turn = ns_a * gram + dot3(gram_pair, poly_pair)
            gram = ns_a * turn + dot3(halves(turn), poly_pair)
    out_ref[...] = chain * (0.3 * inverse)


def update_kernel(apart, carried, me_ref, chain_ref, first_ref, second_ref, weight_ref, *refs):
    new_w, new_m, copy_any, fresh_v, low_v, os = refs[carried:]
    layer = (me_ref[0] & 1) ^ apart
    steps = os.shape[1]
    size = fresh_v.shape[0] // steps
    cuts = [pl.ds(i * size, size) for i in range(steps)]
    pair = halves(chain_ref[...])

    def send(source, target, sem, start=True):
        copy = pltpu.make_async_copy(source, target, sem)
        copy.start() if start else copy.wait()

    def moments(start):
        for k, ref in enumerate((first_ref, second_ref)):

            @pl.when(layer == k)
            def _():
                for i, cut in enumerate(cuts):
                    send(ref.at[cut], new_m.at[k, cut], os.at[0, i], start)

    moments(True)
    for i, cut in enumerate(cuts):
        moment = jnp.where(layer == 0, first_ref[cut], second_ref[cut])
        fresh = weight_ref[layer, cut] * (1.0 - 0.1 * 0.01) - dot3(halves(moment), pair)
        fresh_v[cut] = fresh
        low_v[cut] = fresh.astype(bf16)
        send(fresh_v.at[cut], new_w.at[layer, cut], os.at[1, i])
        send(low_v.at[cut], copy_any.at[layer, cut], os.at[2, i])
    moments(False)
    for i, cut in enumerate(cuts):
        send(fresh_v.at[cut], new_w.at[layer, cut], os.at[1, i], False)
        send(low_v.at[cut], copy_any.at[layer, cut], os.at[2, i], False)


def cosine_rows(index, width):
    cols = jnp.arange(width, dtype=f32)
    freq = index.astype(f32)[..., None]
    return jnp.sqrt(2.0 / width) * jnp.cos(jnp.pi * freq * (2.0 * cols + 1.0) / (2.0 * width))


def swap(value, narrow, wide=0):
    rows, columns = lax.axis_size("wide"), lax.axis_size("narrow")
    pairs = [
        (i * columns + j, (i ^ wide) * columns + (j ^ narrow))
        for i in range(rows)
        for j in range(columns)
    ]
    return lax.ppermute(value, ("wide", "narrow"), pairs)


def stages():
    bits = [(0, 1 << k) for k in range((lax.axis_size("wide") - 1).bit_length())]
    rest = [(2, 0)] + bits
    return [[(1, 0)]] + [rest[i : i + 2] for i in range(0, len(rest), 2)]


def partners(value, bits):
    found = [value]
    offsets = [(0, 0)]
    for narrow, wide in bits:
        offsets = offsets + [(n ^ narrow, w ^ wide) for n, w in offsets]
    for narrow, wide in offsets[1:]:
        found.append(swap(value, narrow, wide))
    return found


def tree(values):
    while len(values) > 1:
        values = [values[i] + values[i + 1] for i in range(0, len(values), 2)]
    return values[0]


def add_kernel(*refs):
    refs[-1][...] = tree([ref[...] for ref in refs[:-1]])


def add_up(parts):
    return call(
        add_kernel,
        "add",
        jax.ShapeDtypeStruct(parts[0].shape, parts[0].dtype),
        [VMEM] * len(parts),
        VMEM,
        [],
        parts[0].size,
        4 * parts[0].size,
        limit=2,
    )(*parts)


def sum_all(value, works=()):
    works = list(works)
    for bits in stages():
        value = add_up(partners(value, bits))
        if works:
            value = works.pop(0)(value)
    return value


def moments_kernel(count, *refs):
    parts, out = [ref[...] for ref in refs[:-1]], refs[-1]
    mean = tree([part[0:1] for part in parts]) * (1.0 / len(parts))
    square = tree([part[1:2] for part in parts])
    apart = tree([jnp.square(part[0:1] - mean) for part in parts])
    out[0:1] = mean
    out[1:2] = square + count * apart
    out[2:3] = tree([part[2:3] for part in parts])
    out[3:8] = jnp.zeros((5, mean.shape[1]), f32)


def merge_moments(stats, count, works=()):
    works = list(works)
    for bits in stages():
        if works:
            stats = works.pop(0)(stats)
        parts = partners(stats, bits)
        stats = call(
            functools.partial(moments_kernel, count),
            "moments",
            jax.ShapeDtypeStruct(stats.shape, f32),
            [VMEM] * len(parts),
            VMEM,
            [],
            stats.size,
            4 * stats.size,
            limit=2,
        )(*parts)
        count = len(parts) * count
    return stats


def mom_gram_kernel(me_ref, mom_any, keep_ref, send_ref, mom_v, sems):
    odd = me_ref[0] & 1
    copies = []
    for k, layer in enumerate((1 - odd, odd)):
        copies.append(pltpu.make_async_copy(mom_any.at[layer], mom_v.at[k], sems.at[k]))
        copies[-1].start()
    for k, out in enumerate((send_ref, keep_ref)):
        copies[k].wait()
        pair = halves(mom_v[k])
        out[...] = dot3(pair, pair, CONTRACT_ROWS)


def adam_rows(param, grad, first, second, rate, decay):
    first = 0.9 * first + 0.1 * grad
    second = 0.999 * second + 0.001 * grad * grad
    mhat = first / (1.0 - 0.9**STEP)
    vhat = second / (1.0 - 0.999**STEP)
    return param - rate * (mhat / (jnp.sqrt(vhat) + 1e-08) + decay * param), first, second


def adam_kernel(
    s1, s2, vec, vec_m, vec_v, head, head_m, head_v, bias, bias_m, bias_v, *outs
):
    o_vec, o_vec_m, bottom, top, o_head, o_head_m, o_head_v, o_bias, o_bias_m, o_bias_v = outs
    rows = ((s1, 1, bottom), (s1, 0, bottom), (s2, 1, top), (s2, 0, top))
    for i, (sums, at, second) in enumerate(rows):
        new, first, square = adam_rows(
            vec[i : i + 1], sums[at : at + 1], vec_m[i : i + 1], vec_v[i : i + 1], 0.3, 0.0
        )
        o_vec[i : i + 1] = new
        o_vec_m[i : i + 1] = first
        second[i & 1 : (i & 1) + 1] = square
    classes = head.shape[0]
    o_head[...], o_head_m[...], o_head_v[...] = adam_rows(
        head[...], s1[2 : 2 + classes], head_m[...], head_v[...], 0.03, 0.01
    )
    o_bias[...], o_bias_m[...], o_bias_v[...] = adam_rows(
        bias[...], s1[2 + classes : 3 + classes, 0:classes], bias_m[...], bias_v[...], 0.3, 0.0
    )


def call(kernel, name, outs, in_specs, out_specs, scratch, flops, moved, limit=10, **more):
    return pl.pallas_call(
        kernel,
        name=name,
        out_shape=outs,
        in_specs=in_specs,
        out_specs=out_specs,
        scratch_shapes=scratch,
        cost_estimate=pl.CostEstimate(flops=flops, bytes_accessed=moved, transcendentals=0),
        compiler_params=pltpu.CompilerParams(vmem_limit_bytes=limit * MIB),
        **more,
    )


def held(*values):
    return [pltpu.with_memory_space_constraint(value, pltpu.VMEM) for value in values]


def dma(n):
    return pltpu.SemaphoreType.DMA((n,))


def per_device(
    images,
    labels,
    class_weight,
    basis_index,
    atom_mask,
    conv_weight,
    conv_momentum,
    batch_norm_params,
    norm_first,
    norm_second,
    head_weight,
    head_first,
    head_second,
    head_bias,
    bias_first,
    bias_second,
):
    count, width = images.shape[0], images.shape[3]
    local_rows = conv_weight.shape[1]
    rank = basis_index.shape[1]
    classes = head_weight.shape[0]
    packed = -(-(classes + 4) // 8) * 8
    wides = lax.axis_size("wide")
    pixel_count = count * PIX * wides * lax.axis_size("narrow")
    me_narrow = lax.axis_index("narrow")
    low_wides = min(8, wides)
    me = jnp.stack([me_narrow, lax.axis_index("wide") & (low_wides - 1)]).astype(jnp.int32)
    sds = jax.ShapeDtypeStruct
    field16 = pltpu.VMEM((PIX, count, width), bf16)
    field32 = (pltpu.VMEM((SIDE, count, width), f32),) * SIDE
    small = sds((8, width), f32)
    weight_v = pltpu.VMEM((TAPS * width, width), bf16)
    conv_flops = 2 * 100 * count * width * width
    field_bytes = 4 * PIX * count * width

    low_weight = conv_weight.astype(bf16)

    def tie(*values):
        return lax.optimization_barrier(values)

    own = low_weight[0]
    near, far = swap(own, 1), swap(own, 2)
    x = images.reshape(count, PIX, width).transpose(1, 0, 2)
    onehot = labels[:, None] == jnp.arange(classes, dtype=jnp.int32)[None, :]
    weight_sum = jnp.sum(jnp.where(onehot, class_weight.astype(f32)[None, :], 0.0))
    extra = jnp.full((1, width), weight_sum, f32)
    bases = cosine_rows(basis_index, width)
    basis_top = bases.astype(bf16)
    basis_rest = (bases - basis_top.astype(f32)).astype(bf16)
    masks = atom_mask[:, 0].transpose(0, 2, 1).astype(bf16)
    head_low = jnp.pad(head_weight.astype(bf16), ((0, 128 - classes), (0, 0)))
    head_bias_row = jnp.pad(head_bias, (0, 128 - classes))[None]
    class_row = jnp.pad(class_weight.astype(f32), (0, 128 - classes))[None]
    prepared = (
        [low_weight[1], masks[0], masks[1]]
        + [basis_top[0], basis_top[1], basis_rest[0], basis_rest[1], basis_top, basis_rest]
        + [head_low, head_bias_row, class_row, labels[None]]
        + [row[None] for row in (head_bias, bias_first, bias_second)]
    )
    gram_keep, gram_send = call(
        mom_gram_kernel,
        "mom_gram",
        (sds((width, width), f32),) * 2,
        [SMEM, ANY],
        (VMEM, VMEM),
        [pltpu.VMEM((2, local_rows, width), f32), dma(2)],
        12 * local_rows * width * width,
        8 * local_rows * width,
        limit=8,
    )(me, pltpu.with_memory_space_constraint(conv_momentum, pltpu.HBM))
    x, extra, me, far, prepared, gram_keep, gram_send = tie(
        x, extra, me, far, prepared, gram_keep, gram_send
    )
    first_weight = (own, near, far, swap(far, 1))
    gram_mine = add_up([gram_keep, swap(gram_send, 1)])
    second_own, mask0, mask1, top0, top1, rest0, rest1, bases_top, bases_rest = prepared[:9]
    head_low, head_bias_row, class_row, label_row, bias_row, bias_m_row, bias_v_row = prepared[9:]
    basis_top, basis_rest = (top0, top1), (rest0, rest1)
    second_near, second_far = swap(second_own, 1), swap(second_own, 2)

    *hid1, stats1 = call(
        conv_first_kernel,
        "conv_first",
        (*field32, small),
        [SMEM, VMEM, VMEM, ANY, ANY, ANY, ANY],
        (VMEM,) * 5,
        [weight_v, dma(4)],
        conv_flops,
        2 * field_bytes,
        limit=7,
        )(me, extra, x, *first_weight)
    hid1 = held(*hid1)
    late = {}

    def last_weight(stats):
        stats, late["far"] = tie(stats, second_far)
        late["last"] = swap(late["far"], 1)
        return stats

    stats1 = merge_moments(stats1, count * PIX, (lambda s: s, lambda s: s, last_weight))

    stats1, gram_mine = tie(stats1, gram_mine)
    gram_other = swap(gram_mine, 2)
    second_weight = (second_own, second_near, late["far"], late["last"])

    outs = call(
        functools.partial(conv_second_kernel, pixel_count),
        "conv_second",
        (*field32, field16, *(pltpu.VMEM((3, width, width), bf16),) * 3, small),
        [SMEM] + [VMEM] * 6 + [ANY] * 4,
        (VMEM,) * 9,
        [weight_v, dma(4)],
        conv_flops,
        3 * field_bytes,
        limit=7,
        )(me, stats1, batch_norm_params, *hid1, *second_weight)
    hid2, z1, turned_weight = held(*outs[:4]), held(outs[4])[0], held(*outs[5:8])
    stats2 = outs[8]
    stats2 = merge_moments(stats2, count * PIX)
    stats2, gram_other = tie(stats2, gram_other)

    *slope2, dp, sums2, aux = call(
        functools.partial(head_kernel, pixel_count, classes),
        "head",
        (*field32, sds((count, width), f32), small, sds((packed, width), f32)),
        [VMEM] * 11,
        (VMEM,) * 7,
        [
            pltpu.VMEM((count, width), bf16),
            pltpu.VMEM((count, width), f32),
            pltpu.VMEM((count, width), f32),
        ],
        conv_flops // 3,
        3 * field_bytes,
        limit=4,
        )(
        stats2,
        batch_norm_params,
        head_low,
        head_bias_row,
        label_row,
        class_row,
        x,
        *hid2,
    )
    slope2 = held(*slope2)
    sums2 = sum_all(sums2)
    sums2, mask0, mask1 = tie(sums2, mask0, mask1)
    gram_pair = (gram_mine, gram_other)
    mask_parts = [(mask, swap(mask, 1), swap(mask, 2)) for mask in (mask1, mask0)]

    dh2, *dy1, sums1 = call(
        functools.partial(second_grad_kernel, pixel_count),
        "second_grad",
        (field16, *field32, sds((packed, width), f32)),
        [VMEM] * 21,
        (VMEM,) * 6,
        [],
        conv_flops,
        5 * field_bytes,
        input_output_aliases={10 + p: 1 + p for p in range(SIDE)},
        limit=3,
        )(stats1, stats2, sums2, batch_norm_params, dp, aux, *hid2, *slope2, *hid1, *turned_weight)

    dh2, dy1 = held(dh2)[0], held(*dy1)
    sums1, far1, far0 = tie(sums1, mask_parts[0][2], mask_parts[1][2])
    masks = [
        (own, near, far, swap(far, 1))
        for (own, near, _), far in zip(mask_parts[::-1], (far0, far1))
    ]
    rows = rank // low_wides
    depth = low_wides // 2
    def coef_outs(outer):
        inner = 4 * depth // outer
        return (sds((inner, rows, local_rows), f32),) * outer + (
            sds((outer, inner, rows, local_rows), f32),
        )

    turned_v = pltpu.VMEM((PIX, 2 * rank, count), bf16)
    basis_v = pltpu.VMEM((width, 2 * rank), bf16)
    sum_v = pltpu.VMEM((TAPS, rank, width), f32)
    mask_v = pltpu.VMEM((4, rank, local_rows), bf16)
    coef_v = pltpu.VMEM((4, rank, local_rows), f32)
    results = {}

    def second_top():
        results["top"] = call(
            coef_top_kernel,
            "coef_top",
            sds((TAPS, rank, width), f32),
            [VMEM] * 4,
            VMEM,
            [basis_v, turned_v],
            conv_flops // 4,
            field_bytes,
        limit=3,
        )(basis_top[1], basis_rest[1], dh2, z1)
        return results["top"]

    def second_bottom():
        results["second"] = call(
            coef_bottom_kernel,
            "coef_bottom",
            coef_outs(2),
            [SMEM] + [VMEM] * 5 + [ANY] * 4,
            (VMEM,) * 3,
            [basis_v, turned_v, sum_v, mask_v, coef_v, dma(4)],
            conv_flops // 4,
            field_bytes,
            limit=9,
        )(me, basis_top[1], basis_rest[1], results["top"], dh2, z1, *masks[1])
        return results["second"]

    def core_stage(outs):
        *keeps, send = outs
        return call(
            add_parts_kernel,
            "add_parts",
            [sds(keep.shape, f32) for keep in keeps],
            [VMEM] * (len(keeps) + 1),
            [VMEM] * len(keeps),
            [],
            rank * local_rows * 2,
            rank * local_rows * 24,
        )(*keeps, swap(send, 1))

    def reduce_stage(parts, offsets, cuts, after=()):
        received = [swap(part, *bits) for part, bits in zip(parts[1:], offsets[1:])]
        received, _ = tie(received, after)
        size = parts[0].shape[0] // cuts
        return call(
            functools.partial(add_pieces_kernel, len(parts)),
            "add_pieces",
            [sds((size, rows, local_rows), f32)] * cuts,
            [VMEM] * len(parts),
            [VMEM] * cuts,
            [],
            rank * local_rows,
            rank * local_rows * 12,
        )(parts[0], *received)

    def high_bits(own):
        own = own.reshape(rows, local_rows)
        bit = low_wides
        while bit < wides:
            own = add_up([own, swap(own, 0, bit)])
            bit = 2 * bit
        return own

    def spread(own):
        found = {0: own}
        for z in range(1, depth):
            found[2 * z] = swap(own, 0, 2 * z)
        found[1] = swap(own, 0, 1)
        for z in range(1, depth):
            found[2 * z + 1] = swap(found[2 * z], 0, 1)
        return [found[k] for k in range(low_wides)]

    def gram_stage(pieces, layer):
        parts = call(
            functools.partial(gram_parts_kernel, layer, low_wides),
            "gram_parts",
            sds((rank, width), f32),
            [SMEM] + [VMEM] * (3 + low_wides),
            VMEM,
            [pltpu.VMEM((rank, local_rows), f32)],
            6 * rank * local_rows * (width + rank),
            4 * local_rows * width,
        )(me, basis_top[layer], basis_rest[layer], conv_momentum, *pieces)
        return parts, swap(parts, 1)

    whole = sds((2, local_rows, width), f32)
    block_v = pltpu.VMEM((local_rows, width), f32)

    def moment_stage(pieces, layer):
        return call(
            functools.partial(moment_kernel, layer, low_wides),
            "moment",
            sds((local_rows, width), f32),
            [SMEM] + [VMEM] * (3 + low_wides),
            VMEM,
            [pltpu.VMEM((rank, local_rows), f32)],
            6 * local_rows * width * rank,
            8 * local_rows * width,
        )(me, basis_top[layer], basis_rest[layer], conv_momentum, *pieces)

    def update_stage(apart, chain, previous):
        carried = len(previous)
        return call(
            functools.partial(update_kernel, apart, carried),
            "update",
            (whole, whole, sds((2, local_rows, width), bf16)),
            [SMEM] + [VMEM] * 4 + [ANY] * carried,
            (ANY,) * 3,
            [block_v, pltpu.VMEM((local_rows, width), bf16), pltpu.SemaphoreType.DMA((3, 3))],
            6 * local_rows * width * width,
            16 * local_rows * width,
            limit=16,
            input_output_aliases={5 + i: i for i in range(carried)},
        )(me, chain, moment1, moment2, conv_weight, *previous)

    def second_core(value):
        value, results["parts"] = tie(value, core_stage(results["second"]))
        return value

    def second_both(value):
        second_top()
        value, results["second"] = tie(value, second_bottom())
        return value

    sums1 = sum_all(sums1, (second_both, second_core))
    first = call(
        functools.partial(coef_first_kernel, pixel_count),
        "coef_first",
        coef_outs(4),
        [SMEM] + [VMEM] * 14 + [ANY] * 4,
        (VMEM,) * 5,
        [basis_v, turned_v, sum_v, mask_v, coef_v, dma(4)],
        conv_flops // 2,
        3 * field_bytes,
        limit=9,
    )(me, basis_top[0], basis_rest[0], stats1, sums1, batch_norm_params, x, *dy1, *hid1, *masks[0])

    parts1 = core_stage(first)
    parts2 = results["parts"]
    pieces1 = reduce_stage(parts1, PLANE, 4)
    pieces2 = reduce_stage(parts2, NEAR, 4, pieces1)
    (own1,) = reduce_stage(pieces1, DEPTH, 1)
    halves2 = reduce_stage(pieces2, PLANE, 2)
    own1 = high_bits(own1)
    all1 = spread(own1)
    (own2,) = reduce_stage(halves2, FAR, 1, own1)
    own2 = high_bits(own2)
    all2 = spread(own2)
    grams2 = gram_stage(all2, 1)
    row, pair, column = sds((4, width), f32), sds((2, width), f32), sds((classes, width), f32)
    line = sds((1, classes), f32)
    small_outs = call(
        adam_kernel,
        "adam",
        (row, row, pair, pair, column, column, column, line, line, line),
        [VMEM] * 11,
        (VMEM,) * 10,
        [],
        100 * classes * width,
        40 * classes * width,
        limit=2,
    )(
        sums1,
        sums2,
        batch_norm_params,
        norm_first,
        norm_second,
        head_weight,
        head_first,
        head_second,
        bias_row,
        bias_m_row,
        bias_v_row,
    )
    small_outs = (*small_outs, sums1[3 + classes, 0], stats1[2, 0])
    moment2 = moment_stage(all2, 1)
    grams1 = gram_stage(all1, 0)
    mine = call(
        pick_kernel,
        "pick",
        sds((rank, width), f32),
        [SMEM] + [VMEM] * 4,
        VMEM,
        [],
        rank * width,
        20 * rank * width,
        limit=4,
    )(me, *grams1, *grams2)
    other = swap(mine, 2)
    moment1 = moment_stage(all1, 0)
    other, moment1, moment2, small_outs = tie(other, moment1, moment2, small_outs)
    chain = call(
        chain_kernel,
        "chain",
        sds((width, width), f32),
        [SMEM] + [VMEM] * 6,
        VMEM,
        [],
        6 * 17 * width**3,
        8 * width * width,
        limit=24,
    )(me, *gram_pair, mine, other, bases_top, bases_rest)
    far_chain = swap(chain, 1)
    outs = update_stage(0, chain, ())
    new_weight, moment, low_copy = update_stage(1, far_chain, outs)

    vec, vec_m, bottom, top, head_new, head_m, head_v, bias_new, bias_m, bias_v = small_outs[:10]
    return (
        small_outs[10],
        small_outs[11],
        new_weight,
        moment,
        low_copy,
        vec,
        vec_m,
        bottom,
        top,
        head_new,
        head_m,
        head_v,
        bias_new[0],
        bias_m[0],
        bias_v[0],
    )


def solution(mesh):
    rep = P()
    rows = P(None, "narrow", None)
    return jax.shard_map(
        per_device,
        mesh=mesh,
        in_specs=(
            P(("wide", "narrow"), None, None, None),
            P(("wide", "narrow")),
            rep,
            rep,
            P(None, "wide", "narrow", None),
            rows,
            rows,
        )
        + (rep,) * 9,
        out_specs=(rep, rep, rows, rows, rows) + (rep,) * 10,
        check_vma=False,
    )
```
